512 devices in a mesh: mem: 8 (over x, core), sp: 64 (over z, y).
Axes of the slice: x: 4, y: 8, z: 8, core: 2. Of those that a mesh axis runs over, the one named last changes fastest.
Arguments:
- control: float32 [16, 256, 512], P('mem', 'sp'), may hold values from -6 to 6
- gradient: float32 [16, 256, 512], P('mem', 'sp'), may hold values from -6 to 6
- direction: float32 [16, 256, 512], P('mem', 'sp'), may hold values from -6 to 6
- perturb: bfloat16 [16, 2, 3072, 1536], P('mem', None, 'sp'), may hold values from -6 to 6
- obs_index: int32 [64, 2048], P('sp'), may hold values from 0 to 147455
- obs_count: int32 [64], P('sp'), may hold values from 1024 to 2048, as said below
- obs_weight: float32 [64, 2048], P('sp'), may hold values from 50 to 800
- cutoff: int32 [1], replicated, may hold values from 24 to 64
Outputs:
- control_new: float32 [16, 256, 512], P('mem', 'sp')
- gradient_new: float32 [16, 256, 512], P('mem', 'sp')
- direction_new: float32 [16, 256, 512], P('mem', 'sp')
The draws below stay inside these ranges and needn't reach their ends.
Inputs may be any that keep to these rules, and one draw needn't show every extreme that they name: `obs_count`: at least one pencil uses all 2048 slots; every pencil uses at least half of them.
All inputs are finite; a program needn't handle non-finite values.
Results may differ from the reference program's by a relative error of at most 0.00035.
Values sent between devices are 32-bit elements; how exact they have to be, the bound alone decides.
No kernel may reach another device: no remote copies, remote signals or barrier semaphores. Data moves between devices by JAX's collectives and lax.ppermute only.
A program may use at most 64 MiB of HBM per device.

```python
import math
import jax
import jax.numpy as jnp
from jax import lax

NA = 3072
NB = 1536
KA = 256
KB = 128
LEVELS = 2
OBS_DEV = 2048
MEMBERS = 16
PENCILS = 64
ROWS = 48
N_SP = 64


def draw_obs_count(key, part):
    key = jax.random.fold_in(key, 11)
    first_key, second_key = jax.random.split(key)
    counts = jax.random.randint(first_key, (PENCILS,), OBS_DEV // 2, OBS_DEV + 1)
    fullest = jax.random.randint(second_key, (), 0, PENCILS)
    return jnp.where(jnp.arange(PENCILS) == fullest, OBS_DEV, counts).astype(jnp.int32)


def place_ends(drawn, key, least, high):
    place = [jax.random.randint(jax.random.fold_in(key, axis), (), 0, length) for axis, length in enumerate(drawn.shape)]
    widest = drawn.shape.index(max(drawn.shape))
    neighbour = place[:widest] + [(place[widest] + 1) % drawn.shape[widest]] + place[widest + 1:]
    return drawn.at[tuple(place)].set(least).at[tuple(neighbour)].set(high)


def shard_levels(stream_key, extent, cuts, low, largest):
    def one(dim, shards_of):
        draws = jax.random.uniform(jax.random.fold_in(jax.random.fold_in(stream_key, 6), dim), (shards_of,), jnp.float32, low / len(cuts), largest / len(cuts))
        return jnp.repeat(jnp.exp(draws), extent[dim] // shards_of).reshape((-1,) + (1,) * (len(extent) - dim - 1))

    level = one(*cuts[0])
    for cut in cuts[1:]:
        level = level * one(*cut)
    return level


def normal_values(stream_key, dims, spread, bound, shards=(), kind=jnp.bfloat16):
    gain = shard_levels(stream_key, dims, shards, -0.22, 0.18) if shards else 1.0
    drawn = jax.random.normal(stream_key, dims, jnp.float32) * spread * gain
    return jnp.minimum(jnp.maximum(drawn, -bound), bound).astype(kind)


def setup_inputs(seed: int = 0) -> dict:
    streams_of = jax.random.split(jax.random.key(seed), 9)
    control = normal_values(streams_of[0], (MEMBERS, 2 * KB, 2 * KA), 1.0, 6.0, ((0, 8), (1, 64)), jnp.float32)
    gradient = normal_values(streams_of[1], (MEMBERS, 2 * KB, 2 * KA), 1.0, 6.0, ((0, 8), (1, 64)), jnp.float32)
    direction = normal_values(streams_of[2], (MEMBERS, 2 * KB, 2 * KA), 1.0, 6.0, ((0, 8), (1, 64)), jnp.float32)
    perturb = normal_values(streams_of[3], (MEMBERS, LEVELS, NA, NB), 1.0, 6.0, ((0, 8), (2, 64)))
    obs_index = place_ends(jax.random.randint(streams_of[4], (PENCILS, OBS_DEV), 0, LEVELS * ROWS * NB), jax.random.fold_in(streams_of[4], 1), 0, (LEVELS * ROWS * NB) - 1).astype(jnp.int32)
    obs_count = draw_obs_count(jax.random.fold_in(streams_of[8], 71), 0)
    obs_weight = jnp.clip(jnp.exp(math.log(800.0) - 2.7725887 * jax.random.uniform(streams_of[6], (PENCILS, OBS_DEV), jnp.float32) ** shard_levels(streams_of[6], (PENCILS, OBS_DEV), ((0, 64),), -0.2, 0.2)), 50.0, 800.0)
    cutoff = jax.random.randint(streams_of[7], (1,), 24, 65).astype(jnp.int32)
    return dict(control=control, gradient=gradient, direction=direction, perturb=perturb, obs_index=obs_index, obs_count=obs_count, obs_weight=obs_weight, cutoff=cutoff)


highest_mode = lax.Precision.HIGHEST

def wave_number(modes):
    column = jnp.arange(2 * modes, dtype=jnp.int32)
    return jnp.where(column < modes, column, column - modes + 1)

def basis_table(points, modes, offset, length):
    grid_row = (offset + jnp.arange(points, dtype=jnp.int32))[:, None]
    column = jnp.arange(2 * modes, dtype=jnp.int32)[None, :]
    wavenum = jnp.where(column < modes, column, column - modes + 1)
    residue = wavenum * grid_row % length
    phase_angle = 2.0 * math.pi / length * residue.astype(jnp.float32)
    return jnp.where(column < modes, jnp.cos(phase_angle), jnp.sin(phase_angle))

def amplitude(cutoff, modes_a, modes_b):
    wave_a = wave_number(modes_a)[None, :]
    wave_b = wave_number(modes_b)[:, None]
    radius = wave_a * wave_a + 4 * wave_b * wave_b
    retained = 4096 * radius <= cutoff[0] * cutoff[0] * modes_a * modes_a
    shape_factor = 1.0 / (1.0 + 16.0 / (modes_a * modes_a) * radius.astype(jnp.float32))
    masked = jnp.where(retained, shape_factor, jnp.zeros_like(shape_factor))
    energy = jnp.sum(masked * masked)
    return masked * jnp.sqrt(2.0 / energy)

def reference(control, gradient, direction, perturb, obs_index, obs_count, obs_weight, cutoff):
    amp = amplitude(cutoff, KA, KB)
    table_a = basis_table(NA, KA, 0, NA)
    second_table = basis_table(NB, KB, 0, NB)
    member_scale = 1.0 / math.sqrt(MEMBERS - 1)

    def forward(total, inputs):
        coeffs, grid_fields = inputs
        spectral = amp * coeffs
        partial_a = jnp.dot(spectral, table_a.T, precision=highest_mode)
        grid_field = jnp.dot(partial_a.T, second_table.T, precision=highest_mode)
        return (total + grid_fields.astype(jnp.float32) * grid_field[None], None)
    increment, _ = lax.scan(forward, jnp.zeros((LEVELS, NA, NB), jnp.float32), (direction, perturb))
    increment = increment * member_scale
    row_count = NA // N_SP
    pencils = increment.reshape(LEVELS, N_SP, row_count, NB).transpose(1, 0, 2, 3).reshape(N_SP, LEVELS * row_count * NB)
    sampled = jnp.take_along_axis(pencils, obs_index, axis=1)
    usable = jnp.arange(OBS_DEV, dtype=jnp.int32)[None, :] < obs_count[:, None]
    weighted = jnp.where(usable, obs_weight * sampled, jnp.zeros_like(sampled))
    pencil_ids = jnp.broadcast_to(jnp.arange(N_SP, dtype=jnp.int32)[:, None], obs_index.shape)
    adjoint_vector_flat = jnp.zeros_like(pencils).at[pencil_ids, obs_index].add(weighted)
    adjoint_field = adjoint_vector_flat.reshape(N_SP, LEVELS, row_count, NB).transpose(1, 0, 2, 3).reshape(LEVELS, NA, NB)

    def backward(inputs):
        coeffs, grid_fields = inputs
        reduced_total = lax.optimization_barrier(jnp.sum(grid_fields.astype(jnp.float32) * adjoint_field, axis=0)) * member_scale
        partial_sum_second = jnp.dot(reduced_total, second_table, precision=highest_mode)
        return coeffs + amp * jnp.dot(partial_sum_second.T, table_a, precision=highest_mode)
    product = lax.map(backward, (direction, perturb))
    grad_sq = jnp.sum(gradient * gradient)
    curvature = jnp.sum(direction * product)
    step_length = grad_sq / curvature
    control_new = control + step_length * direction
    gradient_new = gradient + step_length * product
    new_sq = jnp.sum(gradient_new * gradient_new)
    direction_new = -gradient_new + new_sq / grad_sq * direction
    return (control_new, gradient_new, direction_new)
```

```python
import functools
import math

import jax
import jax.numpy as jnp
import numpy as np
from jax import lax
from jax.experimental import pallas as pl
from jax.experimental.pallas import tpu as pltpu
from jax.sharding import PartitionSpec as P

NA, NB, KA, KB = 3072, 1536, 256, 128
LEVELS, SLOTS, MEMBERS, ROWS, N_SP = 2, 2048, 16, 48, 64
LOCAL_M, LOCAL_KB = 2, 4
SIDE = 8
SCALE = 1.0 / math.sqrt(MEMBERS - 1)
CHUNK = LOCAL_KB * LOCAL_M * ROWS

f32, bf16, i32 = jnp.float32, jnp.bfloat16, jnp.int32
VMEM = pl.BlockSpec(memory_space=pltpu.VMEM)
HBM = pl.BlockSpec(memory_space=pltpu.HBM)
SMEM = pl.BlockSpec(memory_space=pltpu.SMEM)
PARAMS = pltpu.CompilerParams(vmem_limit_bytes=40 * 1024 * 1024)
WHOLE = pltpu.CompilerParams(vmem_limit_bytes=60 * 1024 * 1024)


def tables():
    w = np.arange(KA, dtype=np.int64)
    s = np.arange(N_SP, dtype=np.int64)[:, None]
    turn = 2.0 * np.pi * ((s * w) % N_SP) / N_SP
    r = np.arange(ROWS, dtype=np.int64)[:, None]
    ws = np.where(w == 0, KA, w)
    cos_rows = np.cos(2.0 * np.pi * ((r * w) % NA) / NA)
    sin_rows = np.sin(2.0 * np.pi * ((r * ws) % NA) / NA)
    rows = np.concatenate([cos_rows, sin_rows], axis=1).astype(np.float32)
    high = rows.astype(jnp.bfloat16)
    low = (rows - high.astype(np.float32)).astype(jnp.bfloat16)
    phase = np.stack([np.cos(turn), np.sin(turn)]).astype(np.float32)
    return phase, np.stack([high, low])


def split(x):
    high = x.astype(bf16)
    return high, (x - high.astype(f32)).astype(bf16)


def dot(a, b, dims):
    return lax.dot_general(a, b, (dims, ((), ())), preferred_element_type=f32)


def wave(column, modes):
    return jnp.where(column < modes, column, column - modes + 1)


def shape_factor(radius, cutoff):
    retained = 4096 * radius <= cutoff * cutoff * (KA * KA)
    factor = 1.0 / (1.0 + (16.0 / (KA * KA)) * radius.astype(f32))
    return jnp.where(retained, factor, 0.0)


def to_rows(cut_ref, pen_ref, dir_in, phase_in, rows_in, out_ref, amp_ref, high_ref, low_ref, dir_ref, phase_ref,
            rows_ref, sems):
    pairs = ((dir_in, dir_ref), (phase_in, phase_ref), (rows_in, rows_ref))
    copies = [pltpu.make_async_copy(a, b, sems.at[i]) for i, (a, b) in enumerate(pairs)]
    for copy in copies:
        copy.start()
    cutoff, pencil = cut_ref[0], pen_ref[0]
    wa = lax.broadcasted_iota(i32, (1, 384), 1)
    wb = lax.broadcasted_iota(i32, (136, 1), 0)
    count_a = jnp.where(wa > KA, 0.0, jnp.where((wa == 0) | (wa == KA), 1.0, 2.0))
    count_b = jnp.where(wb > KB, 0.0, jnp.where((wb == 0) | (wb == KB), 1.0, 2.0))
    factor = shape_factor(wa * wa + 4 * (wb * wb), cutoff)
    energy = jnp.sum(factor * factor * count_a * count_b, axis=0, keepdims=True)
    energy = jnp.sum(energy, axis=1, keepdims=True)
    gain = jnp.sqrt(2.0 / energy)
    wa = wave(lax.broadcasted_iota(i32, (1, 2 * KA), 1), KA)
    wb = wave(lax.broadcasted_iota(i32, (LOCAL_KB, 1), 0) + pencil * LOCAL_KB, KB)
    amp = shape_factor(wa * wa + 4 * (wb * wb), cutoff) * gain
    amp_ref[...] = amp

    for copy in copies:
        copy.wait()
    phase_c, phase_s = phase_ref[0], phase_ref[1]
    for m in range(LOCAL_M):
        spectral = amp * dir_ref[m]
        part_c = spectral[:, :KA]
        part_s = pltpu.roll(spectral[:, KA:], 1, 1)
        for k in range(LOCAL_KB):
            c, s = part_c[k:k + 1], part_s[k:k + 1]
            at = pl.ds((k * LOCAL_M + m) * N_SP, N_SP)
            for half, value in ((0, c * phase_c + s * phase_s), (1, s * phase_c - c * phase_s)):
                high, low = split(value)
                high_ref[at, half * KA:(half + 1) * KA] = high
                low_ref[at, half * KA:(half + 1) * KA] = low
    nt = ((1,), (1,))
    result = (dot(high_ref[...], rows_ref[0], nt) + dot(high_ref[...], rows_ref[1], nt)
              + dot(low_ref[...], rows_ref[0], nt))
    for i in range(LOCAL_M * LOCAL_KB):
        out_ref[:, 0, i * ROWS:(i + 1) * ROWS] = result[i * N_SP:(i + 1) * N_SP]


def cell_parts(index_ref):
    index = index_ref[...]
    line = jnp.floor((index.astype(f32) + 0.5) * (1.0 / NB)).astype(i32)
    column = index - line * NB
    return line, column


def turns_to_cos_sin(turns):
    quarter = jnp.floor(turns * 4.0 + 0.5)
    x = (turns - quarter * 0.25) * (2.0 * math.pi)
    x2 = x * x
    s = x * (1.0 + x2 * (-1.0 / 6 + x2 * (1.0 / 120 + x2 * (-1.0 / 5040 + x2 * (1.0 / 362880)))))
    c = 1.0 + x2 * (-0.5 + x2 * (1.0 / 24 + x2 * (-1.0 / 720 + x2 * (1.0 / 40320))))
    q = quarter.astype(i32) & 3
    odd = (q & 1) == 1
    cos = jnp.where(odd, s, c)
    sin = jnp.where(odd, c, s)
    return jnp.where((q == 1) | (q == 2), -cos, cos), jnp.where(q >= 2, -sin, sin)


def residue_turns(wavenum, column):
    product = wavenum * column
    return (product - jnp.floor(product * (1.0 / NB)) * NB) * (1.0 / NB)


def at_slots(index_ref, pert_ref, basis_ref, values_ref):
    block = 256

    @pl.loop(0, SLOTS // block)
    def _(step):
        at = pl.ds(pl.multiple_of(step * block, block), block)
        index = index_ref[:, at]
        line = jnp.floor((index.astype(f32) + 0.5) * (1.0 / NB)).astype(i32)
        column = index - line * NB
        place = column.astype(f32)
        y = lax.broadcasted_iota(i32, (SIDE, 1), 0)
        cos_y, sin_y = turns_to_cos_sin(residue_turns((4 * y).astype(f32), place))
        q = lax.broadcasted_iota(i32, (SIDE * LOCAL_KB, 1), 0)
        is_sin = (q & 7) >= SIDE // 2
        wq = (32 * (q & 3) + (q >> 3) + is_sin.astype(i32)).astype(f32)
        cos_q, sin_q = turns_to_cos_sin(residue_turns(wq, place) - jnp.where(is_sin, 0.25, 0.0))
        for pair in range(SIDE * LOCAL_KB // 2):
            both = [cos_y * cos_q[g:g + 1] - sin_y * sin_q[g:g + 1] for g in (2 * pair, 2 * pair + 1)]
            high, low = split(jnp.concatenate(both, axis=0))
            basis_ref[0, pair * 16:(pair + 1) * 16, at] = high
            basis_ref[1, pair * 16:(pair + 1) * 16, at] = low
        lines = LEVELS * ROWS
        grid_column = lax.broadcasted_iota(i32, (NB, block), 0)
        chosen = jnp.where(grid_column == column, 1.0, 0.0).astype(bf16)
        found = dot(pert_ref[...], chosen, ((1,), (0,)))
        mine = lax.broadcasted_iota(i32, (lines, block), 0) == line
        for m in range(LOCAL_M):
            part = jnp.where(mine, found[m * lines:(m + 1) * lines], 0.0)
            values_ref[m:m + 1, at] = jnp.sum(part, axis=0, keepdims=True)


def sample(recv_ref, basis_ref, values_ref, index_ref, out_ref):
    wide = LOCAL_M * ROWS
    field = jnp.concatenate([recv_ref[:, 0, k * wide:(k + 1) * wide] for k in range(LOCAL_KB)], axis=0)
    high, low = split(field.T)
    nn = ((1,), (0,))
    both = dot(jnp.concatenate([high, low], axis=0), basis_ref[0], nn)
    rows = both[:wide] + both[wide:] + dot(high, basis_ref[1], nn)
    line, _ = cell_parts(index_ref)
    row = jnp.where(line >= ROWS, line - ROWS, line)
    mine = lax.broadcasted_iota(i32, (ROWS, SLOTS), 0) == row
    total = jnp.zeros((1, SLOTS), f32)
    for m in range(LOCAL_M):
        part = jnp.sum(jnp.where(mine, rows[m * ROWS:(m + 1) * ROWS], 0.0), axis=0, keepdims=True)
        total += values_ref[m:m + 1] * part
    out_ref[...] = total * SCALE


def spread(count_ref, parts_ref, weight_ref, basis_ref, values_ref, index_ref, out_ref):
    sampled = jnp.sum(parts_ref[...], axis=0)
    usable = lax.broadcasted_iota(i32, (1, SLOTS), 1) < count_ref[0]
    weighted = jnp.where(usable, weight_ref[...] * sampled, 0.0) * SCALE
    line, _ = cell_parts(index_ref)
    row = jnp.where(line >= ROWS, line - ROWS, line)
    mine = lax.broadcasted_iota(i32, (ROWS, SLOTS), 0) == row
    highs, lows = [], []
    for m in range(LOCAL_M):
        value = values_ref[m:m + 1] * weighted
        high = value.astype(bf16).astype(f32)
        highs.append(jnp.where(mine, high, 0.0).astype(bf16))
        lows.append(jnp.where(mine, value - high, 0.0).astype(bf16))
    empty = jnp.zeros((32, SLOTS), bf16)
    right = jnp.concatenate(highs + [empty] + lows + [empty], axis=0)
    nt = ((1,), (1,))
    both = dot(basis_ref[0], right, nt)
    result = both[:, :128] + both[:, 128:] + dot(basis_ref[1], right[:128], nt)
    wide = LOCAL_M * ROWS
    for k in range(LOCAL_KB):
        out_ref[:, 0, k * wide:(k + 1) * wide] = result[k * N_SP:(k + 1) * N_SP, :wide]


def fold(x):
    x = jnp.sum(x, axis=0, keepdims=True)
    return x[:, :128] + x[:, 128:256] + x[:, 256:384] + x[:, 384:]


def from_rows(recv_ref, phase_ref, rows_ref, amp_ref, dir_ref, grad_ref, prod_ref, sums_ref):
    count = LOCAL_M * LOCAL_KB
    left = jnp.concatenate([recv_ref[:, 0, i * ROWS:(i + 1) * ROWS] for i in range(count)], axis=0)
    high, low = split(left)
    nn = ((1,), (0,))
    turned = dot(high, rows_ref[0], nn) + dot(high, rows_ref[1], nn) + dot(low, rows_ref[0], nn)
    phase_c, phase_s = phase_ref[0], phase_ref[1]
    amp = amp_ref[...]
    totals = [jnp.zeros((1, 128), f32)] * 4
    for m in range(LOCAL_M):
        part_c, part_s = [], []
        for k in range(LOCAL_KB):
            i = k * LOCAL_M + m
            p, q = turned[i * N_SP:(i + 1) * N_SP, :KA], turned[i * N_SP:(i + 1) * N_SP, KA:]
            part_c.append(jnp.sum(p * phase_c - q * phase_s, axis=0, keepdims=True))
            part_s.append(jnp.sum(p * phase_s + q * phase_c, axis=0, keepdims=True))
        back_c = jnp.concatenate(part_c, axis=0)
        back_s = pltpu.roll(jnp.concatenate(part_s, axis=0), KA - 1, 1)
        d, g = dir_ref[m], grad_ref[m]
        product = d + amp * jnp.concatenate([back_c, back_s], axis=1)
        prod_ref[m] = product
        terms = (g * g, d * product, g * product, product * product)
        totals = [t + fold(x) for t, x in zip(totals, terms)]
    sums = jnp.concatenate(totals + [jnp.zeros((4, 128), f32)], axis=0)
    sums_ref[...] = sums


def update(parts_ref, cont_ref, grad_ref, dir_ref, prod_ref, cont_out, grad_out, dir_out):
    sums = jnp.sum(jnp.sum(parts_ref[...], axis=0), axis=1, keepdims=True)
    grad_sq, curvature, cross, prod_sq = [sums[i:i + 1] for i in range(4)]
    step = grad_sq / curvature
    new_sq = grad_sq + step * (2.0 * cross + step * prod_sq)
    ratio = new_sq / grad_sq
    for m in range(LOCAL_M):
        d = dir_ref[m]
        fresh = grad_ref[m] + step * prod_ref[m]
        cont_out[m] = cont_ref[m] + step * d
        grad_out[m] = fresh
        dir_out[m] = ratio * d - fresh


def call(kernel, in_specs, outs, scratch=(), flops=0, moved=0, params=PARAMS):
    shapes = [jax.ShapeDtypeStruct(shape, dtype) for shape, dtype in outs]
    return pl.pallas_call(
        kernel,
        out_shape=shapes,
        in_specs=in_specs,
        out_specs=[VMEM] * len(shapes),
        scratch_shapes=list(scratch),
        compiler_params=params,
        cost_estimate=pl.CostEstimate(flops=flops, bytes_accessed=moved, transcendentals=0),
    )


def stage_to_rows(cutoff, pencil, direction, phase, rows):
    return call(
        to_rows, [SMEM, SMEM, HBM, HBM, HBM],
        [((N_SP, 1, CHUNK), f32), ((LOCAL_KB, 2 * KA), f32)],
        [pltpu.VMEM((8 * N_SP, 2 * KA), bf16), pltpu.VMEM((8 * N_SP, 2 * KA), bf16),
         pltpu.VMEM((LOCAL_M, LOCAL_KB, 2 * KA), f32), pltpu.VMEM((2, N_SP, KA), f32),
         pltpu.VMEM((2, ROWS, 2 * KA), bf16), pltpu.SemaphoreType.DMA((3,))],
        flops=10 ** 8, moved=10 ** 6, params=WHOLE,
    )(cutoff, pencil, direction, phase, rows)


def stage_at_slots(index, perturb):
    return call(
        at_slots, [VMEM, VMEM],
        [((2, 2 * KB, SLOTS), bf16), ((LOCAL_M, SLOTS), f32)],
        flops=2 * 10 ** 9, moved=4 * 10 ** 6,
    )(index, perturb)


def stage_sample(recv, basis, values, index):
    return call(
        sample, [VMEM] * 4, [((1, SLOTS), f32)], flops=3 * 10 ** 8, moved=2 * 10 ** 6,
    )(recv, basis, values, index)[0]


def stage_spread(count, parts, weight, basis, values, index):
    return call(
        spread, [SMEM] + [VMEM] * 5, [((N_SP, 1, CHUNK), f32)], flops=3 * 10 ** 8, moved=2 * 10 ** 6,
    )(count, parts, weight, basis, values, index)[0]


def stage_from_rows(recv, phase, rows, amp, direction, gradient):
    return call(
        from_rows, [VMEM] * 6,
        [((LOCAL_M, LOCAL_KB, 2 * KA), f32), ((SIDE, 128), f32)],
        flops=10 ** 8, moved=10 ** 6,
    )(recv, phase, rows, amp, direction, gradient)


def stage_update(parts, control, gradient, direction, product):
    shape = (LOCAL_M, LOCAL_KB, 2 * KA)
    return call(
        update, [VMEM] * 5, [(shape, f32)] * 3, flops=10 ** 5, moved=10 ** 5,
    )(parts, control, gradient, direction, product)


def swap(x):
    return lax.all_to_all(x, "sp", 0, 0, tiled=True)


def shards(phase, rows, control, gradient, direction, perturb, obs_index, obs_count, obs_weight, cutoff):
    pencil = lax.axis_index("sp").astype(i32).reshape(1)
    send, amp = stage_to_rows(cutoff, pencil, direction, phase, rows)
    basis, values = stage_at_slots(obs_index, perturb.reshape(LOCAL_M * LEVELS * ROWS, NB))
    part = stage_sample(swap(send), basis, values, obs_index)
    parts = lax.all_gather(part, "mem")
    send = stage_spread(obs_count, parts, obs_weight, basis, values, obs_index)
    product, sums = stage_from_rows(swap(send), phase, rows, amp, direction, gradient)
    sums = jnp.sum(lax.all_gather(sums, "mem"), axis=0)
    sums = lax.all_gather(sums, "sp")
    return tuple(stage_update(sums, control, gradient, direction, product))


def solution(mesh):
    spectral = P("mem", "sp", None)
    placed = (spectral, spectral, spectral, P("mem", None, "sp", None), P("sp", None), P("sp"), P("sp", None), P())
    phase, rows = tables()
    return jax.shard_map(
        functools.partial(shards, phase, rows),
        mesh=mesh,
        in_specs=placed,
        out_specs=(spectral, spectral, spectral),
        check_vma=False,
    )
```

```python
import functools
import math

import jax
import jax.numpy as jnp
import numpy as np
from jax import lax
from jax.experimental import pallas as pl
from jax.experimental.pallas import tpu as pltpu
from jax.sharding import PartitionSpec as P

NA, NB, KA, KB = 3072, 1536, 256, 128
LEVELS, SLOTS, MEMBERS, ROWS, N_SP = 2, 2048, 16, 48, 64
LOCAL_M, LOCAL_KB = 2, 4
SIDE = 8
SCALE = 1.0 / math.sqrt(MEMBERS - 1)
CHUNK = LOCAL_KB * LOCAL_M * ROWS

f32, bf16, i32 = jnp.float32, jnp.bfloat16, jnp.int32
VMEM = pl.BlockSpec(memory_space=pltpu.VMEM)
HBM = pl.BlockSpec(memory_space=pltpu.HBM)
SMEM = pl.BlockSpec(memory_space=pltpu.SMEM)
PARAMS = pltpu.CompilerParams(vmem_limit_bytes=40 * 1024 * 1024)
WHOLE = pltpu.CompilerParams(vmem_limit_bytes=60 * 1024 * 1024)


def tables():
    w = np.arange(KA, dtype=np.int64)
    s = np.arange(N_SP, dtype=np.int64)[:, None]
    turn = 2.0 * np.pi * ((s * w) % N_SP) / N_SP
    r = np.arange(ROWS, dtype=np.int64)[:, None]
    ws = np.where(w == 0, KA, w)
    cos_rows = np.cos(2.0 * np.pi * ((r * w) % NA) / NA)
    sin_rows = np.sin(2.0 * np.pi * ((r * ws) % NA) / NA)
    rows = np.concatenate([cos_rows, sin_rows], axis=1).astype(np.float32)
    phase = np.stack([np.cos(turn), np.sin(turn)]).astype(np.float32)
    return phase, rows


def split(x):
    high = x.astype(bf16)
    return high, (x - high.astype(f32)).astype(bf16)


def dot(a, b, dims):
    return lax.dot_general(a, b, (dims, ((), ())), preferred_element_type=f32)


def wave(column, modes):
    return jnp.where(column < modes, column, column - modes + 1)


def shape_factor(radius, cutoff):
    retained = 4096 * radius <= cutoff * cutoff * (KA * KA)
    factor = 1.0 / (1.0 + (16.0 / (KA * KA)) * radius.astype(f32))
    return jnp.where(retained, factor, 0.0)


def to_rows(pen_ref, cut_ref, dir_in, out_ref, amp_ref, high_ref, low_ref, dir_ref, sem):
    dir_copy = pltpu.make_async_copy(dir_in, dir_ref, sem)
    dir_copy.start()
    w = lax.broadcasted_iota(i32, (1, KA), 1)
    s = lax.broadcasted_iota(i32, (N_SP, 1), 0)
    phase_c, phase_s = turns_to_cos_sin(((s * w) & (N_SP - 1)).astype(f32) * (1.0 / N_SP))
    r = lax.broadcasted_iota(i32, (ROWS, 1), 0)
    slot = lax.broadcasted_iota(i32, (1, 2 * KA), 1)
    ws = jnp.where(slot < KA, slot, jnp.where(slot == KA, KA, slot - KA))
    cos_r, sin_r = turns_to_cos_sin(residue_turns(ws.astype(f32), r.astype(f32), NA))
    table_high, table_low = split(jnp.where(slot < KA, cos_r, sin_r))
    cutoff, pencil = cut_ref[0], pen_ref[0]
    wa = lax.broadcasted_iota(i32, (1, 384), 1)
    wb = lax.broadcasted_iota(i32, (136, 1), 0)
    count_a = jnp.where(wa > KA, 0.0, jnp.where((wa == 0) | (wa == KA), 1.0, 2.0))
    count_b = jnp.where(wb > KB, 0.0, jnp.where((wb == 0) | (wb == KB), 1.0, 2.0))
    factor = shape_factor(wa * wa + 4 * (wb * wb), cutoff)
    energy = jnp.sum(factor * factor * count_a * count_b, axis=0, keepdims=True)
    energy = jnp.sum(energy, axis=1, keepdims=True)
    gain = jnp.sqrt(2.0 / energy)
    wa = wave(lax.broadcasted_iota(i32, (1, 2 * KA), 1), KA)
    wb = wave(lax.broadcasted_iota(i32, (LOCAL_KB, 1), 0) + pencil * LOCAL_KB, KB)
    amp = shape_factor(wa * wa + 4 * (wb * wb), cutoff) * gain
    amp_ref[...] = amp

    dir_copy.wait()
    for m in range(LOCAL_M):
        spectral = amp * dir_ref[m]
        part_c = spectral[:, :KA]
        part_s = pltpu.roll(spectral[:, KA:], 1, 1)
        for k in range(LOCAL_KB):
            c, s = part_c[k:k + 1], part_s[k:k + 1]
            at = pl.ds((k * LOCAL_M + m) * N_SP, N_SP)
            for half, value in ((0, c * phase_c + s * phase_s), (1, s * phase_c - c * phase_s)):
                high, low = split(value)
                high_ref[at, half * KA:(half + 1) * KA] = high
                low_ref[at, half * KA:(half + 1) * KA] = low
    nt = ((1,), (1,))
    result = (dot(high_ref[...], table_high, nt) + dot(high_ref[...], table_low, nt)
              + dot(low_ref[...], table_high, nt))
    for i in range(LOCAL_M * LOCAL_KB):
        out_ref[:, 0, i * ROWS:(i + 1) * ROWS] = result[i * N_SP:(i + 1) * N_SP]


def cell_parts(index_ref):
    index = index_ref[...]
    line = jnp.floor((index.astype(f32) + 0.5) * (1.0 / NB)).astype(i32)
    column = index - line * NB
    return line, column


def turns_to_cos_sin(turns):
    quarter = jnp.floor(turns * 4.0 + 0.5)
    x = (turns - quarter * 0.25) * (2.0 * math.pi)
    x2 = x * x
    s = x * (1.0 + x2 * (-1.0 / 6 + x2 * (1.0 / 120 + x2 * (-1.0 / 5040 + x2 * (1.0 / 362880)))))
    c = 1.0 + x2 * (-0.5 + x2 * (1.0 / 24 + x2 * (-1.0 / 720 + x2 * (1.0 / 40320))))
    q = quarter.astype(i32) & 3
    odd = (q & 1) == 1
    cos = jnp.where(odd, s, c)
    sin = jnp.where(odd, c, s)
    return jnp.where((q == 1) | (q == 2), -cos, cos), jnp.where(q >= 2, -sin, sin)


def residue_turns(wavenum, place, length):
    product = wavenum * place
    return (product - jnp.floor(product * (1.0 / length)) * length) * (1.0 / length)


def at_slots(count_ref, index_ref, weight_ref, pert_ref, basis_ref, values_ref, masked_ref):
    block = 256
    usable = lax.broadcasted_iota(i32, (1, SLOTS), 1) < count_ref[0]
    masked_ref[...] = jnp.where(usable, weight_ref[...] * (SCALE * SCALE), 0.0)

    @pl.loop(0, SLOTS // block)
    def _(step):
        at = pl.ds(pl.multiple_of(step * block, block), block)
        index = index_ref[:, at]
        line = jnp.floor((index.astype(f32) + 0.5) * (1.0 / NB)).astype(i32)
        column = index - line * NB
        place = column.astype(f32)
        y = lax.broadcasted_iota(i32, (SIDE, 1), 0)
        cos_y, sin_y = turns_to_cos_sin(residue_turns((4 * y).astype(f32), place, NB))
        q = lax.broadcasted_iota(i32, (SIDE * LOCAL_KB, 1), 0)
        is_sin = (q & 7) >= SIDE // 2
        wq = (32 * (q & 3) + (q >> 3) + is_sin.astype(i32)).astype(f32)
        cos_q, sin_q = turns_to_cos_sin(residue_turns(wq, place, NB) - jnp.where(is_sin, 0.25, 0.0))
        for pair in range(SIDE * LOCAL_KB // 2):
            both = [cos_y * cos_q[g:g + 1] - sin_y * sin_q[g:g + 1] for g in (2 * pair, 2 * pair + 1)]
            high, low = split(jnp.concatenate(both, axis=0))
            basis_ref[0, pair * 16:(pair + 1) * 16, at] = high
            basis_ref[1, pair * 16:(pair + 1) * 16, at] = low
        lines = LEVELS * ROWS
        grid_column = lax.broadcasted_iota(i32, (NB, block), 0)
        chosen = jnp.where(grid_column == column, 1.0, 0.0).astype(bf16)
        found = dot(pert_ref[...], chosen, ((1,), (0,)))
        mine = lax.broadcasted_iota(i32, (lines, block), 0) == line
        for m in range(LOCAL_M):
            part = jnp.where(mine, found[m * lines:(m + 1) * lines], 0.0)
            values_ref[m:m + 1, at] = jnp.sum(part, axis=0, keepdims=True)


def sample(recv_ref, basis_ref, values_ref, index_ref, out_ref):
    wide = LOCAL_M * ROWS
    field = jnp.concatenate([recv_ref[:, 0, k * wide:(k + 1) * wide] for k in range(LOCAL_KB)], axis=0)
    high, low = split(field.T)
    nn = ((1,), (0,))
    both = dot(jnp.concatenate([high, low], axis=0), basis_ref[0], nn)
    rows = both[:wide] + both[wide:] + dot(high, basis_ref[1], nn)
    line, _ = cell_parts(index_ref)
    row = jnp.where(line >= ROWS, line - ROWS, line)
    mine = lax.broadcasted_iota(i32, (ROWS, SLOTS), 0) == row
    total = jnp.zeros((1, SLOTS), f32)
    for m in range(LOCAL_M):
        part = jnp.sum(jnp.where(mine, rows[m * ROWS:(m + 1) * ROWS], 0.0), axis=0, keepdims=True)
        total += values_ref[m:m + 1] * part
    out_ref[...] = jnp.concatenate([total[:, i * 128:(i + 1) * 128] for i in range(SLOTS // 128)], axis=0)


def spread(parts_ref, masked_ref, basis_ref, values_ref, index_ref, out_ref):
    sampled = jnp.sum(parts_ref[...], axis=0)
    sampled = jnp.concatenate([sampled[i:i + 1] for i in range(SLOTS // 128)], axis=1)
    weighted = masked_ref[...] * sampled
    line, _ = cell_parts(index_ref)
    row = jnp.where(line >= ROWS, line - ROWS, line)
    mine = lax.broadcasted_iota(i32, (ROWS, SLOTS), 0) == row
    highs, lows = [], []
    for m in range(LOCAL_M):
        value = values_ref[m:m + 1] * weighted
        high = value.astype(bf16).astype(f32)
        highs.append(jnp.where(mine, high, 0.0).astype(bf16))
        lows.append(jnp.where(mine, value - high, 0.0).astype(bf16))
    empty = jnp.zeros((32, SLOTS), bf16)
    right = jnp.concatenate(highs + [empty] + lows + [empty], axis=0)
    nt = ((1,), (1,))
    both = dot(basis_ref[0], right, nt)
    result = both[:, :128] + both[:, 128:] + dot(basis_ref[1], right[:128], nt)
    wide = LOCAL_M * ROWS
    for k in range(LOCAL_KB):
        out_ref[:, 0, k * wide:(k + 1) * wide] = result[k * N_SP:(k + 1) * N_SP, :wide]


def fold(x):
    x = jnp.sum(x, axis=0, keepdims=True)
    return x[:, :128] + x[:, 128:256] + x[:, 256:384] + x[:, 384:]


def from_rows(recv_ref, phase_ref, rows_ref, amp_ref, dir_ref, grad_ref, prod_ref, sums_ref):
    count = LOCAL_M * LOCAL_KB
    left = jnp.concatenate([recv_ref[:, 0, i * ROWS:(i + 1) * ROWS] for i in range(count)], axis=0)
    high, low = split(left)
    nn = ((1,), (0,))
    table_high, table_low = split(rows_ref[...])
    turned = dot(high, table_high, nn) + dot(high, table_low, nn) + dot(low, table_high, nn)
    phase_c, phase_s = phase_ref[0], phase_ref[1]
    amp = amp_ref[...]
    totals = [jnp.zeros((1, 128), f32)] * 4
    for m in range(LOCAL_M):
        part_c, part_s = [], []
        for k in range(LOCAL_KB):
            i = k * LOCAL_M + m
            p, q = turned[i * N_SP:(i + 1) * N_SP, :KA], turned[i * N_SP:(i + 1) * N_SP, KA:]
            part_c.append(jnp.sum(p * phase_c - q * phase_s, axis=0, keepdims=True))
            part_s.append(jnp.sum(p * phase_s + q * phase_c, axis=0, keepdims=True))
        back_c = jnp.concatenate(part_c, axis=0)
        back_s = pltpu.roll(jnp.concatenate(part_s, axis=0), KA - 1, 1)
        d, g = dir_ref[m], grad_ref[m]
        product = d + amp * jnp.concatenate([back_c, back_s], axis=1)
        prod_ref[m] = product
        terms = (g * g, d * product, g * product, product * product)
        totals = [t + fold(x) for t, x in zip(totals, terms)]
    lane = lax.broadcasted_iota(i32, (1, 128), 1)
    line = jnp.zeros((1, 128), f32)
    for k, t in enumerate(totals):
        t = t + pltpu.roll(t, 64, 1)
        t = t + pltpu.roll(t, 32, 1)
        line = jnp.where((lane >> 5) == k, t, line)
    sums_ref[...] = line


def update(parts_ref, cont_ref, grad_ref, dir_ref, prod_ref, cont_out, grad_out, dir_out):
    line = jnp.sum(parts_ref[...], axis=0)
    group = lax.broadcasted_iota(i32, (1, 128), 1) >> 5
    grad_sq, curvature, cross, prod_sq = [
        jnp.sum(jnp.where(group == k, line, 0.0), axis=1, keepdims=True) for k in range(4)]
    step = grad_sq / curvature
    new_sq = grad_sq + step * (2.0 * cross + step * prod_sq)
    ratio = new_sq / grad_sq
    for m in range(LOCAL_M):
        d = dir_ref[m]
        fresh = grad_ref[m] + step * prod_ref[m]
        cont_out[m] = cont_ref[m] + step * d
        grad_out[m] = fresh
        dir_out[m] = ratio * d - fresh


def call(kernel, in_specs, outs, scratch=(), flops=0, moved=0, params=PARAMS):
    shapes = [jax.ShapeDtypeStruct(shape, dtype) for shape, dtype in outs]
    return pl.pallas_call(
        kernel,
        out_shape=shapes,
        in_specs=in_specs,
        out_specs=[VMEM] * len(shapes),
        scratch_shapes=list(scratch),
        compiler_params=params,
        cost_estimate=pl.CostEstimate(flops=flops, bytes_accessed=moved, transcendentals=0),
    )


def stage_to_rows(pencil, cutoff, direction):
    return call(
        to_rows, [SMEM, SMEM, HBM],
        [((N_SP, 1, CHUNK), f32), ((LOCAL_KB, 2 * KA), f32)],
        [pltpu.VMEM((8 * N_SP, 2 * KA), bf16), pltpu.VMEM((8 * N_SP, 2 * KA), bf16),
         pltpu.VMEM((LOCAL_M, LOCAL_KB, 2 * KA), f32), pltpu.SemaphoreType.DMA],
        flops=10 ** 8, moved=10 ** 6, params=WHOLE,
    )(pencil, cutoff, direction)


def stage_at_slots(count, index, weight, perturb):
    return call(
        at_slots, [SMEM] + [VMEM] * 3,
        [((2, 2 * KB, SLOTS), bf16), ((LOCAL_M, SLOTS), f32), ((1, SLOTS), f32)],
        flops=2 * 10 ** 9, moved=4 * 10 ** 6,
    )(count, index, weight, perturb)


def stage_sample(recv, basis, values, index):
    return call(
        sample, [VMEM] * 4, [((SLOTS // 128, 128), f32)], flops=3 * 10 ** 8, moved=2 * 10 ** 6,
    )(recv, basis, values, index)[0]


def stage_spread(parts, masked, basis, values, index):
    return call(
        spread, [VMEM] * 5, [((N_SP, 1, CHUNK), f32)], flops=3 * 10 ** 8, moved=2 * 10 ** 6,
    )(parts, masked, basis, values, index)[0]


def stage_from_rows(recv, phase, rows, amp, direction, gradient):
    return call(
        from_rows, [VMEM] * 6,
        [((LOCAL_M, LOCAL_KB, 2 * KA), f32), ((1, 128), f32)],
        flops=10 ** 8, moved=10 ** 6,
    )(recv, phase, rows, amp, direction, gradient)


def stage_update(parts, control, gradient, direction, product):
    shape = (LOCAL_M, LOCAL_KB, 2 * KA)
    return call(
        update, [VMEM] * 5, [(shape, f32)] * 3, flops=10 ** 5, moved=10 ** 5,
    )(parts, control, gradient, direction, product)


NEAR = [[m * N_SP + s + y for m in range(SIDE) for y in range(4)] for s in range(0, N_SP, 4)]
FAR = [[m * N_SP + s + y for s in range(0, N_SP, 4)] for m in range(SIDE) for y in range(4)]


def swap(x):
    return lax.all_to_all(x, "sp", 0, 0, tiled=True)


def share(x, axis, count, groups=None):
    x = jnp.broadcast_to(x[None], (count,) + x.shape)
    return lax.all_to_all(x, axis, 0, 0, axis_index_groups=groups, tiled=True)


def shards(phase, rows, control, gradient, direction, perturb, obs_index, obs_count, obs_weight, cutoff):
    pencil = lax.axis_index("sp").astype(i32).reshape(1)
    send, amp = stage_to_rows(pencil, cutoff, direction)
    basis, values, masked = stage_at_slots(
        obs_count, obs_index, obs_weight, perturb.reshape(LOCAL_M * LEVELS * ROWS, NB))
    part = stage_sample(swap(send), basis, values, obs_index)
    send = stage_spread(share(part, "mem", SIDE), masked, basis, values, obs_index)
    product, sums = stage_from_rows(swap(send), phase, rows, amp, direction, gradient)
    sums = jnp.sum(share(sums, ("mem", "sp"), len(NEAR[0]), NEAR), axis=0)
    sums = share(sums, ("mem", "sp"), len(FAR[0]), FAR)
    return tuple(stage_update(sums, control, gradient, direction, product))


def solution(mesh):
    spectral = P("mem", "sp", None)
    placed = (spectral, spectral, spectral, P("mem", None, "sp", None), P("sp", None), P("sp"), P("sp", None), P())
    phase, rows = tables()
    return jax.shard_map(
        functools.partial(shards, phase, rows),
        mesh=mesh,
        in_specs=placed,
        out_specs=(spectral, spectral, spectral),
        check_vma=False,
    )
```

```python
import functools
import math

import jax
import jax.numpy as jnp
import numpy as np
from jax import lax
from jax.experimental import pallas as pl
from jax.experimental.pallas import tpu as pltpu
from jax.sharding import PartitionSpec as P

NA, NB, KA, KB = 3072, 1536, 256, 128
LEVELS, SLOTS, MEMBERS, ROWS, N_SP = 2, 2048, 16, 48, 64
LOCAL_M, LOCAL_KB = 2, 4
SIDE = 8
SCALE = 1.0 / math.sqrt(MEMBERS - 1)
CHUNK = LOCAL_KB * LOCAL_M * ROWS

f32, bf16, i32 = jnp.float32, jnp.bfloat16, jnp.int32
VMEM = pl.BlockSpec(memory_space=pltpu.VMEM)
HBM = pl.BlockSpec(memory_space=pltpu.HBM)
SMEM = pl.BlockSpec(memory_space=pltpu.SMEM)
PARAMS = pltpu.CompilerParams(vmem_limit_bytes=40 * 1024 * 1024)
WHOLE = pltpu.CompilerParams(vmem_limit_bytes=60 * 1024 * 1024)


def tables():
    w = np.arange(KA, dtype=np.int64)
    s = np.arange(N_SP, dtype=np.int64)[:, None]
    turn = 2.0 * np.pi * ((s * w) % N_SP) / N_SP
    r = np.arange(ROWS, dtype=np.int64)[:, None]
    ws = np.where(w == 0, KA, w)
    cos_rows = np.cos(2.0 * np.pi * ((r * w) % NA) / NA)
    sin_rows = np.sin(2.0 * np.pi * ((r * ws) % NA) / NA)
    rows = np.concatenate([cos_rows, sin_rows], axis=1).astype(np.float32)
    phase = np.stack([np.cos(turn), np.sin(turn)]).astype(np.float32)
    return phase, rows


def split(x):
    high = x.astype(bf16)
    return high, (x - high.astype(f32)).astype(bf16)


def dot(a, b, dims):
    return lax.dot_general(a, b, (dims, ((), ())), preferred_element_type=f32)


def wave(column, modes):
    return jnp.where(column < modes, column, column - modes + 1)


def shape_factor(radius, cutoff):
    retained = 4096 * radius <= cutoff * cutoff * (KA * KA)
    factor = 1.0 / (1.0 + (16.0 / (KA * KA)) * radius.astype(f32))
    return jnp.where(retained, factor, 0.0)


def to_rows(pen_ref, cut_ref, dir_in, out_ref, amp_ref, high_ref, low_ref, dir_ref, sem):
    dir_copy = pltpu.make_async_copy(dir_in, dir_ref, sem)
    dir_copy.start()
    w = lax.broadcasted_iota(i32, (1, KA), 1)
    s = lax.broadcasted_iota(i32, (N_SP, 1), 0)
    phase_c, phase_s = turns_to_cos_sin(((s * w) & (N_SP - 1)).astype(f32) * (1.0 / N_SP))
    r = lax.broadcasted_iota(i32, (ROWS, 1), 0)
    slot = lax.broadcasted_iota(i32, (1, 2 * KA), 1)
    ws = jnp.where(slot < KA, slot, jnp.where(slot == KA, KA, slot - KA))
    cos_r, sin_r = turns_to_cos_sin(residue_turns(ws.astype(f32), r.astype(f32), NA))
    table_high, table_low = split(jnp.where(slot < KA, cos_r, sin_r))
    cutoff, pencil = cut_ref[0], pen_ref[0]
    wa = lax.broadcasted_iota(i32, (1, 384), 1)
    wb = lax.broadcasted_iota(i32, (136, 1), 0)
    count_a = jnp.where(wa > KA, 0.0, jnp.where((wa == 0) | (wa == KA), 1.0, 2.0))
    count_b = jnp.where(wb > KB, 0.0, jnp.where((wb == 0) | (wb == KB), 1.0, 2.0))
    factor = shape_factor(wa * wa + 4 * (wb * wb), cutoff)
    energy = jnp.sum(factor * factor * count_a * count_b, axis=0, keepdims=True)
    energy = jnp.sum(energy, axis=1, keepdims=True)
    gain = jnp.sqrt(2.0 / energy)
    wa = wave(lax.broadcasted_iota(i32, (1, 2 * KA), 1), KA)
    wb = wave(lax.broadcasted_iota(i32, (LOCAL_KB, 1), 0) + pencil * LOCAL_KB, KB)
    amp = shape_factor(wa * wa + 4 * (wb * wb), cutoff) * gain
    amp_ref[...] = amp

    dir_copy.wait()
    for m in range(LOCAL_M):
        spectral = amp * dir_ref[m]
        part_c = spectral[:, :KA]
        part_s = pltpu.roll(spectral[:, KA:], 1, 1)
        for k in range(LOCAL_KB):
            c, s = part_c[k:k + 1], part_s[k:k + 1]
            at = pl.ds((k * LOCAL_M + m) * N_SP, N_SP)
            for half, value in ((0, c * phase_c + s * phase_s), (1, s * phase_c - c * phase_s)):
                high, low = split(value)
                high_ref[at, half * KA:(half + 1) * KA] = high
                low_ref[at, half * KA:(half + 1) * KA] = low
    nt = ((1,), (1,))
    result = (dot(high_ref[...], table_high, nt) + dot(high_ref[...], table_low, nt)
              + dot(low_ref[...], table_high, nt))
    pieces = [result[i * N_SP:(i + 1) * N_SP] for i in range(LOCAL_M * LOCAL_KB)]
    out_ref[:, 0, :] = jnp.concatenate(pieces, axis=1)


def cell_parts(index_ref):
    index = index_ref[...]
    line = jnp.floor((index.astype(f32) + 0.5) * (1.0 / NB)).astype(i32)
    column = index - line * NB
    return line, column


def turns_to_cos_sin(turns):
    quarter = jnp.floor(turns * 4.0 + 0.5)
    x = (turns - quarter * 0.25) * (2.0 * math.pi)
    x2 = x * x
    s = x * (1.0 + x2 * (-1.0 / 6 + x2 * (1.0 / 120 + x2 * (-1.0 / 5040 + x2 * (1.0 / 362880)))))
    c = 1.0 + x2 * (-0.5 + x2 * (1.0 / 24 + x2 * (-1.0 / 720 + x2 * (1.0 / 40320))))
    q = quarter.astype(i32) & 3
    odd = (q & 1) == 1
    cos = jnp.where(odd, s, c)
    sin = jnp.where(odd, c, s)
    return jnp.where((q == 1) | (q == 2), -cos, cos), jnp.where(q >= 2, -sin, sin)


def residue_turns(wavenum, place, length):
    product = wavenum * place
    return (product - jnp.floor(product * (1.0 / length)) * length) * (1.0 / length)


def at_slots(count_ref, index_ref, weight_ref, pert_ref, basis_ref, values_ref, masked_ref):
    block = 256
    usable = lax.broadcasted_iota(i32, (1, SLOTS), 1) < count_ref[0]
    masked_ref[...] = jnp.where(usable, weight_ref[...] * (SCALE * SCALE), 0.0)

    @pl.loop(0, SLOTS // block)
    def _(step):
        at = pl.ds(pl.multiple_of(step * block, block), block)
        index = index_ref[:, at]
        line = jnp.floor((index.astype(f32) + 0.5) * (1.0 / NB)).astype(i32)
        column = index - line * NB
        place = column.astype(f32)
        y = lax.broadcasted_iota(i32, (SIDE, 1), 0)
        cos_y, sin_y = turns_to_cos_sin(residue_turns((4 * y).astype(f32), place, NB))
        q = lax.broadcasted_iota(i32, (SIDE * LOCAL_KB, 1), 0)
        is_sin = (q & 7) >= SIDE // 2
        wq = (32 * (q & 3) + (q >> 3) + is_sin.astype(i32)).astype(f32)
        cos_q, sin_q = turns_to_cos_sin(residue_turns(wq, place, NB) - jnp.where(is_sin, 0.25, 0.0))
        for pair in range(SIDE * LOCAL_KB // 2):
            both = [cos_y * cos_q[g:g + 1] - sin_y * sin_q[g:g + 1] for g in (2 * pair, 2 * pair + 1)]
            high, low = split(jnp.concatenate(both, axis=0))
            basis_ref[0, pair * 16:(pair + 1) * 16, at] = high
            basis_ref[1, pair * 16:(pair + 1) * 16, at] = low
        lines = LEVELS * ROWS
        grid_column = lax.broadcasted_iota(i32, (NB, block), 0)
        chosen = jnp.where(grid_column == column, 1.0, 0.0).astype(bf16)
        found = dot(pert_ref[...], chosen, ((1,), (0,)))
        mine = lax.broadcasted_iota(i32, (lines, block), 0) == line
        for m in range(LOCAL_M):
            part = jnp.where(mine, found[m * lines:(m + 1) * lines], 0.0)
            values_ref[m:m + 1, at] = jnp.sum(part, axis=0, keepdims=True)


def sample(recv_ref, basis_ref, values_ref, index_ref, out_ref):
    wide = LOCAL_M * ROWS
    recv = recv_ref[:, 0, :]
    field = jnp.concatenate([recv[:, k * wide:(k + 1) * wide] for k in range(LOCAL_KB)], axis=0)
    high, low = split(field.T)
    nn = ((1,), (0,))
    both = dot(jnp.concatenate([high, low], axis=0), basis_ref[0], nn)
    rows = both[:wide] + both[wide:] + dot(high, basis_ref[1], nn)
    line, _ = cell_parts(index_ref)
    row = jnp.where(line >= ROWS, line - ROWS, line)
    mine = lax.broadcasted_iota(i32, (ROWS, SLOTS), 0) == row
    total = jnp.zeros((1, SLOTS), f32)
    for m in range(LOCAL_M):
        part = jnp.sum(jnp.where(mine, rows[m * ROWS:(m + 1) * ROWS], 0.0), axis=0, keepdims=True)
        total += values_ref[m:m + 1] * part
    out_ref[...] = jnp.concatenate([total[:, i * 128:(i + 1) * 128] for i in range(SLOTS // 128)], axis=0)


def spread(parts_ref, masked_ref, basis_ref, values_ref, index_ref, out_ref):
    sampled = jnp.sum(parts_ref[...], axis=0)
    sampled = jnp.concatenate([sampled[i:i + 1] for i in range(SLOTS // 128)], axis=1)
    weighted = masked_ref[...] * sampled
    line, _ = cell_parts(index_ref)
    row = jnp.where(line >= ROWS, line - ROWS, line)
    mine = lax.broadcasted_iota(i32, (ROWS, SLOTS), 0) == row
    highs, lows = [], []
    for m in range(LOCAL_M):
        value = values_ref[m:m + 1] * weighted
        high = value.astype(bf16).astype(f32)
        highs.append(jnp.where(mine, high, 0.0).astype(bf16))
        lows.append(jnp.where(mine, value - high, 0.0).astype(bf16))
    empty = jnp.zeros((32, SLOTS), bf16)
    right = jnp.concatenate(highs + [empty] + lows + [empty], axis=0)
    nt = ((1,), (1,))
    both = dot(basis_ref[0], right, nt)
    result = both[:, :128] + both[:, 128:] + dot(basis_ref[1], right[:128], nt)
    wide = LOCAL_M * ROWS
    pieces = [result[k * N_SP:(k + 1) * N_SP, :wide] for k in range(LOCAL_KB)]
    out_ref[:, 0, :] = jnp.concatenate(pieces, axis=1)


def fold(x):
    x = jnp.sum(x, axis=0, keepdims=True)
    return x[:, :128] + x[:, 128:256] + x[:, 256:384] + x[:, 384:]


def from_rows(recv_ref, phase_ref, rows_ref, amp_ref, dir_ref, grad_ref, prod_ref, sums_ref):
    count = LOCAL_M * LOCAL_KB
    recv = recv_ref[:, 0, :]
    left = jnp.concatenate([recv[:, i * ROWS:(i + 1) * ROWS] for i in range(count)], axis=0)
    high, low = split(left)
    nn = ((1,), (0,))
    table_high, table_low = split(rows_ref[...])
    turned = dot(high, table_high, nn) + dot(high, table_low, nn) + dot(low, table_high, nn)
    phase_c, phase_s = phase_ref[0], phase_ref[1]
    amp = amp_ref[...]
    totals = [jnp.zeros((1, 128), f32)] * 4
    for m in range(LOCAL_M):
        part_c, part_s = [], []
        for k in range(LOCAL_KB):
            i = k * LOCAL_M + m
            p, q = turned[i * N_SP:(i + 1) * N_SP, :KA], turned[i * N_SP:(i + 1) * N_SP, KA:]
            part_c.append(jnp.sum(p * phase_c - q * phase_s, axis=0, keepdims=True))
            part_s.append(jnp.sum(p * phase_s + q * phase_c, axis=0, keepdims=True))
        back_c = jnp.concatenate(part_c, axis=0)
        back_s = pltpu.roll(jnp.concatenate(part_s, axis=0), KA - 1, 1)
        d, g = dir_ref[m], grad_ref[m]
        product = d + amp * jnp.concatenate([back_c, back_s], axis=1)
        prod_ref[m] = product
        terms = (g * g, d * product, g * product, product * product)
        totals = [t + fold(x) for t, x in zip(totals, terms)]
    lane = lax.broadcasted_iota(i32, (1, 128), 1)
    line = jnp.zeros((1, 128), f32)
    for k, t in enumerate(totals):
        t = t + pltpu.roll(t, 64, 1)
        t = t + pltpu.roll(t, 32, 1)
        line = jnp.where((lane >> 5) == k, t, line)
    sums_ref[...] = line


def update(parts_ref, cont_ref, grad_ref, dir_ref, prod_ref, cont_out, grad_out, dir_out):
    line = jnp.sum(parts_ref[...], axis=0)
    group = lax.broadcasted_iota(i32, (1, 128), 1) >> 5
    grad_sq, curvature, cross, prod_sq = [
        jnp.sum(jnp.where(group == k, line, 0.0), axis=1, keepdims=True) for k in range(4)]
    step = grad_sq / curvature
    new_sq = grad_sq + step * (2.0 * cross + step * prod_sq)
    ratio = new_sq / grad_sq
    for m in range(LOCAL_M):
        d = dir_ref[m]
        fresh = grad_ref[m] + step * prod_ref[m]
        cont_out[m] = cont_ref[m] + step * d
        grad_out[m] = fresh
        dir_out[m] = ratio * d - fresh


def call(kernel, in_specs, outs, scratch=(), flops=0, moved=0, params=PARAMS):
    shapes = [jax.ShapeDtypeStruct(shape, dtype) for shape, dtype in outs]
    return pl.pallas_call(
        kernel,
        out_shape=shapes,
        in_specs=in_specs,
        out_specs=[VMEM] * len(shapes),
        scratch_shapes=list(scratch),
        compiler_params=params,
        cost_estimate=pl.CostEstimate(flops=flops, bytes_accessed=moved, transcendentals=0),
    )


def stage_to_rows(pencil, cutoff, direction):
    return call(
        to_rows, [SMEM, SMEM, HBM],
        [((N_SP, 1, CHUNK), f32), ((LOCAL_KB, 2 * KA), f32)],
        [pltpu.VMEM((8 * N_SP, 2 * KA), bf16), pltpu.VMEM((8 * N_SP, 2 * KA), bf16),
         pltpu.VMEM((LOCAL_M, LOCAL_KB, 2 * KA), f32), pltpu.SemaphoreType.DMA],
        flops=10 ** 8, moved=10 ** 6, params=WHOLE,
    )(pencil, cutoff, direction)


def stage_at_slots(count, index, weight, perturb):
    return call(
        at_slots, [SMEM] + [VMEM] * 3,
        [((2, 2 * KB, SLOTS), bf16), ((LOCAL_M, SLOTS), f32), ((1, SLOTS), f32)],
        flops=2 * 10 ** 9, moved=4 * 10 ** 6,
    )(count, index, weight, perturb)


def stage_sample(recv, basis, values, index):
    return call(
        sample, [VMEM] * 4, [((SLOTS // 128, 128), f32)], flops=3 * 10 ** 8, moved=2 * 10 ** 6,
    )(recv, basis, values, index)[0]


def stage_spread(parts, masked, basis, values, index):
    return call(
        spread, [VMEM] * 5, [((N_SP, 1, CHUNK), f32)], flops=3 * 10 ** 8, moved=2 * 10 ** 6,
    )(parts, masked, basis, values, index)[0]


def stage_from_rows(recv, phase, rows, amp, direction, gradient):
    return call(
        from_rows, [VMEM] * 6,
        [((LOCAL_M, LOCAL_KB, 2 * KA), f32), ((1, 128), f32)],
        flops=10 ** 8, moved=10 ** 6,
    )(recv, phase, rows, amp, direction, gradient)


def stage_update(parts, control, gradient, direction, product):
    shape = (LOCAL_M, LOCAL_KB, 2 * KA)
    return call(
        update, [VMEM] * 5, [(shape, f32)] * 3, flops=10 ** 5, moved=10 ** 5,
    )(parts, control, gradient, direction, product)


NEAR = [[m * N_SP + s + y for m in range(SIDE) for y in range(2)] for s in range(0, N_SP, 2)]
FAR = [[m * N_SP + s + y for s in range(0, N_SP, 2)] for m in range(SIDE) for y in range(2)]


def swap(x):
    return lax.all_to_all(x, "sp", 0, 0, tiled=True)


def share(x, axis, count, groups=None):
    x = jnp.broadcast_to(x[None], (count,) + x.shape)
    return lax.all_to_all(x, axis, 0, 0, axis_index_groups=groups, tiled=True)


def shards(phase, rows, control, gradient, direction, perturb, obs_index, obs_count, obs_weight, cutoff):
    pencil = lax.axis_index("sp").astype(i32).reshape(1)
    send, amp = stage_to_rows(pencil, cutoff, direction)
    basis, values, masked = stage_at_slots(
        obs_count, obs_index, obs_weight, perturb.reshape(LOCAL_M * LEVELS * ROWS, NB))
    part = stage_sample(swap(send), basis, values, obs_index)
    send = stage_spread(share(part, "mem", SIDE), masked, basis, values, obs_index)
    product, sums = stage_from_rows(swap(send), phase, rows, amp, direction, gradient)
    sums = jnp.sum(share(sums, ("mem", "sp"), len(NEAR[0]), NEAR), axis=0)
    sums = share(sums, ("mem", "sp"), len(FAR[0]), FAR)
    return tuple(stage_update(sums, control, gradient, direction, product))


def solution(mesh):
    spectral = P("mem", "sp", None)
    placed = (spectral, spectral, spectral, P("mem", None, "sp", None), P("sp", None), P("sp"), P("sp", None), P())
    phase, rows = tables()
    return jax.shard_map(
        functools.partial(shards, phase, rows),
        mesh=mesh,
        in_specs=placed,
        out_specs=(spectral, spectral, spectral),
        check_vma=False,
    )
```

```python
import functools
import math

import jax
import jax.numpy as jnp
import numpy as np
from jax import lax
from jax.experimental import pallas as pl
from jax.experimental.pallas import tpu as pltpu
from jax.sharding import PartitionSpec as P

NA, NB, KA, KB = 3072, 1536, 256, 128
LEVELS, SLOTS, MEMBERS, ROWS, N_SP = 2, 2048, 16, 48, 64
LOCAL_M, LOCAL_KB = 2, 4
SIDE = 8
SCALE = 1.0 / math.sqrt(MEMBERS - 1)
CHUNK = LOCAL_KB * LOCAL_M * ROWS


def spanned(masks):
    out = [0]
    for mask in masks:
        out += [mask ^ x for x in out]
    return out


ORDER = spanned([63, 45, 44, 37, 16, 58])
PLACE = [ORDER.index(s) for s in range(N_SP)]
NEAR = [[s ^ d for d in spanned([449, 385, 192, 1])] for s in range(0, N_SP, 2)]
FAR = [[m * N_SP + (y ^ d) for d in spanned([62, 46, 52, 54, 6])] for m in range(SIDE) for y in range(2)]

f32, bf16, i32 = jnp.float32, jnp.bfloat16, jnp.int32
VMEM = pl.BlockSpec(memory_space=pltpu.VMEM)
HBM = pl.BlockSpec(memory_space=pltpu.HBM)
SMEM = pl.BlockSpec(memory_space=pltpu.SMEM)
PARAMS = pltpu.CompilerParams(vmem_limit_bytes=40 * 1024 * 1024)
WHOLE = pltpu.CompilerParams(vmem_limit_bytes=60 * 1024 * 1024)


def tables():
    w = np.arange(KA, dtype=np.int64)
    s = np.arange(N_SP, dtype=np.int64)[:, None]
    turn = 2.0 * np.pi * ((s * w) % N_SP) / N_SP
    r = np.arange(ROWS, dtype=np.int64)[:, None]
    ws = np.where(w == 0, KA, w)
    cos_rows = np.cos(2.0 * np.pi * ((r * w) % NA) / NA)
    sin_rows = np.sin(2.0 * np.pi * ((r * ws) % NA) / NA)
    rows = np.concatenate([cos_rows, sin_rows], axis=1).astype(np.float32)
    phase = np.stack([np.cos(turn), np.sin(turn)]).astype(np.float32)
    return phase, rows


def split(x):
    high = x.astype(bf16)
    return high, (x - high.astype(f32)).astype(bf16)


def put_rows(ref, rows):
    for p, s in enumerate(ORDER):
        ref[p] = rows[s:s + 1]


def get_rows(ref):
    return jnp.concatenate([ref[p] for p in PLACE], axis=0)


def dot(a, b, dims):
    return lax.dot_general(a, b, (dims, ((), ())), preferred_element_type=f32)


def wave(column, modes):
    return jnp.where(column < modes, column, column - modes + 1)


def shape_factor(radius, cutoff):
    retained = 4096 * radius <= cutoff * cutoff * (KA * KA)
    factor = 1.0 / (1.0 + (16.0 / (KA * KA)) * radius.astype(f32))
    return jnp.where(retained, factor, 0.0)


def to_rows(pen_ref, cut_ref, dir_in, out_ref, amp_ref, high_ref, low_ref, dir_ref, sem):
    dir_copy = pltpu.make_async_copy(dir_in, dir_ref, sem)
    dir_copy.start()
    w = lax.broadcasted_iota(i32, (1, KA), 1)
    s = lax.broadcasted_iota(i32, (N_SP, 1), 0)
    phase_c, phase_s = turns_to_cos_sin(((s * w) & (N_SP - 1)).astype(f32) * (1.0 / N_SP))
    r = lax.broadcasted_iota(i32, (ROWS, 1), 0)
    slot = lax.broadcasted_iota(i32, (1, 2 * KA), 1)
    ws = jnp.where(slot < KA, slot, jnp.where(slot == KA, KA, slot - KA))
    cos_r, sin_r = turns_to_cos_sin(residue_turns(ws.astype(f32), r.astype(f32), NA))
    table_high, table_low = split(jnp.where(slot < KA, cos_r, sin_r))
    cutoff, pencil = cut_ref[0], pen_ref[0]
    wa = lax.broadcasted_iota(i32, (1, 384), 1)
    wb = lax.broadcasted_iota(i32, (136, 1), 0)
    count_a = jnp.where(wa > KA, 0.0, jnp.where((wa == 0) | (wa == KA), 1.0, 2.0))
    count_b = jnp.where(wb > KB, 0.0, jnp.where((wb == 0) | (wb == KB), 1.0, 2.0))
    factor = shape_factor(wa * wa + 4 * (wb * wb), cutoff)
    energy = jnp.sum(factor * factor * count_a * count_b, axis=0, keepdims=True)
    energy = jnp.sum(energy, axis=1, keepdims=True)
    gain = jnp.sqrt(2.0 / energy)
    wa = wave(lax.broadcasted_iota(i32, (1, 2 * KA), 1), KA)
    wb = wave(lax.broadcasted_iota(i32, (LOCAL_KB, 1), 0) + pencil * LOCAL_KB, KB)
    amp = shape_factor(wa * wa + 4 * (wb * wb), cutoff) * gain
    amp_ref[...] = amp

    dir_copy.wait()
    for m in range(LOCAL_M):
        spectral = amp * dir_ref[m]
        part_c = spectral[:, :KA]
        part_s = pltpu.roll(spectral[:, KA:], 1, 1)
        for k in range(LOCAL_KB):
            c, s = part_c[k:k + 1], part_s[k:k + 1]
            at = pl.ds((k * LOCAL_M + m) * N_SP, N_SP)
            for half, value in ((0, c * phase_c + s * phase_s), (1, s * phase_c - c * phase_s)):
                high, low = split(value)
                high_ref[at, half * KA:(half + 1) * KA] = high
                low_ref[at, half * KA:(half + 1) * KA] = low
    nt = ((1,), (1,))
    result = (dot(high_ref[...], table_high, nt) + dot(high_ref[...], table_low, nt)
              + dot(low_ref[...], table_high, nt))
    pieces = [result[i * N_SP:(i + 1) * N_SP] for i in range(LOCAL_M * LOCAL_KB)]
    put_rows(out_ref, jnp.concatenate(pieces, axis=1))


def cell_parts(index_ref):
    index = index_ref[...]
    line = jnp.floor((index.astype(f32) + 0.5) * (1.0 / NB)).astype(i32)
    column = index - line * NB
    return line, column


def turns_to_cos_sin(turns):
    quarter = jnp.floor(turns * 4.0 + 0.5)
    x = (turns - quarter * 0.25) * (2.0 * math.pi)
    x2 = x * x
    s = x * (1.0 + x2 * (-1.0 / 6 + x2 * (1.0 / 120 + x2 * (-1.0 / 5040 + x2 * (1.0 / 362880)))))
    c = 1.0 + x2 * (-0.5 + x2 * (1.0 / 24 + x2 * (-1.0 / 720 + x2 * (1.0 / 40320))))
    q = quarter.astype(i32) & 3
    odd = (q & 1) == 1
    cos = jnp.where(odd, s, c)
    sin = jnp.where(odd, c, s)
    return jnp.where((q == 1) | (q == 2), -cos, cos), jnp.where(q >= 2, -sin, sin)


def residue_turns(wavenum, place, length):
    product = wavenum * place
    return (product - jnp.floor(product * (1.0 / length)) * length) * (1.0 / length)


def at_slots(count_ref, index_ref, weight_ref, pert_ref, basis_ref, values_ref, masked_ref):
    block = 256
    usable = lax.broadcasted_iota(i32, (1, SLOTS), 1) < count_ref[0]
    masked_ref[...] = jnp.where(usable, weight_ref[...] * (SCALE * SCALE), 0.0)

    @pl.loop(0, SLOTS // block)
    def _(step):
        at = pl.ds(pl.multiple_of(step * block, block), block)
        index = index_ref[:, at]
        line = jnp.floor((index.astype(f32) + 0.5) * (1.0 / NB)).astype(i32)
        column = index - line * NB
        place = column.astype(f32)
        y = lax.broadcasted_iota(i32, (SIDE, 1), 0)
        cos_y, sin_y = turns_to_cos_sin(residue_turns((4 * y).astype(f32), place, NB))
        q = lax.broadcasted_iota(i32, (SIDE * LOCAL_KB, 1), 0)
        is_sin = (q & 7) >= SIDE // 2
        wq = (32 * (q & 3) + (q >> 3) + is_sin.astype(i32)).astype(f32)
        cos_q, sin_q = turns_to_cos_sin(residue_turns(wq, place, NB) - jnp.where(is_sin, 0.25, 0.0))
        for pair in range(SIDE * LOCAL_KB // 2):
            both = [cos_y * cos_q[g:g + 1] - sin_y * sin_q[g:g + 1] for g in (2 * pair, 2 * pair + 1)]
            high, low = split(jnp.concatenate(both, axis=0))
            basis_ref[0, pair * 16:(pair + 1) * 16, at] = high
            basis_ref[1, pair * 16:(pair + 1) * 16, at] = low
        lines = LEVELS * ROWS
        grid_column = lax.broadcasted_iota(i32, (NB, block), 0)
        chosen = jnp.where(grid_column == column, 1.0, 0.0).astype(bf16)
        found = dot(pert_ref[...], chosen, ((1,), (0,)))
        mine = lax.broadcasted_iota(i32, (lines, block), 0) == line
        for m in range(LOCAL_M):
            part = jnp.where(mine, found[m * lines:(m + 1) * lines], 0.0)
            values_ref[m:m + 1, at] = jnp.sum(part, axis=0, keepdims=True)


def sample(recv_ref, basis_ref, values_ref, index_ref, out_ref):
    wide = LOCAL_M * ROWS
    recv = get_rows(recv_ref)
    field = jnp.concatenate([recv[:, k * wide:(k + 1) * wide] for k in range(LOCAL_KB)], axis=0)
    high, low = split(field.T)
    nn = ((1,), (0,))
    both = dot(jnp.concatenate([high, low], axis=0), basis_ref[0], nn)
    rows = both[:wide] + both[wide:] + dot(high, basis_ref[1], nn)
    line, _ = cell_parts(index_ref)
    row = jnp.where(line >= ROWS, line - ROWS, line)
    mine = lax.broadcasted_iota(i32, (ROWS, SLOTS), 0) == row
    total = jnp.zeros((1, SLOTS), f32)
    for m in range(LOCAL_M):
        part = jnp.sum(jnp.where(mine, rows[m * ROWS:(m + 1) * ROWS], 0.0), axis=0, keepdims=True)
        total += values_ref[m:m + 1] * part
    out_ref[...] = jnp.concatenate([total[:, i * 128:(i + 1) * 128] for i in range(SLOTS // 128)], axis=0)


def spread(parts_ref, masked_ref, basis_ref, values_ref, index_ref, out_ref):
    sampled = jnp.sum(parts_ref[...], axis=0)
    sampled = jnp.concatenate([sampled[i:i + 1] for i in range(SLOTS // 128)], axis=1)
    weighted = masked_ref[...] * sampled
    line, _ = cell_parts(index_ref)
    row = jnp.where(line >= ROWS, line - ROWS, line)
    mine = lax.broadcasted_iota(i32, (ROWS, SLOTS), 0) == row
    highs, lows = [], []
    for m in range(LOCAL_M):
        value = values_ref[m:m + 1] * weighted
        high = value.astype(bf16).astype(f32)
        highs.append(jnp.where(mine, high, 0.0).astype(bf16))
        lows.append(jnp.where(mine, value - high, 0.0).astype(bf16))
    empty = jnp.zeros((32, SLOTS), bf16)
    right = jnp.concatenate(highs + [empty] + lows + [empty], axis=0)
    nt = ((1,), (1,))
    both = dot(basis_ref[0], right, nt)
    result = both[:, :128] + both[:, 128:] + dot(basis_ref[1], right[:128], nt)
    wide = LOCAL_M * ROWS
    pieces = [result[k * N_SP:(k + 1) * N_SP, :wide] for k in range(LOCAL_KB)]
    put_rows(out_ref, jnp.concatenate(pieces, axis=1))


def fold(x):
    x = jnp.sum(x, axis=0, keepdims=True)
    return x[:, :128] + x[:, 128:256] + x[:, 256:384] + x[:, 384:]


def from_rows(recv_ref, phase_ref, rows_ref, amp_ref, dir_ref, grad_ref, prod_ref, sums_ref):
    count = LOCAL_M * LOCAL_KB
    recv = get_rows(recv_ref)
    left = jnp.concatenate([recv[:, i * ROWS:(i + 1) * ROWS] for i in range(count)], axis=0)
    high, low = split(left)
    nn = ((1,), (0,))
    table_high, table_low = split(rows_ref[...])
    turned = dot(high, table_high, nn) + dot(high, table_low, nn) + dot(low, table_high, nn)
    phase_c, phase_s = phase_ref[0], phase_ref[1]
    amp = amp_ref[...]
    totals = [jnp.zeros((1, 128), f32)] * 4
    for m in range(LOCAL_M):
        part_c, part_s = [], []
        for k in range(LOCAL_KB):
            i = k * LOCAL_M + m
            p, q = turned[i * N_SP:(i + 1) * N_SP, :KA], turned[i * N_SP:(i + 1) * N_SP, KA:]
            part_c.append(jnp.sum(p * phase_c - q * phase_s, axis=0, keepdims=True))
            part_s.append(jnp.sum(p * phase_s + q * phase_c, axis=0, keepdims=True))
        back_c = jnp.concatenate(part_c, axis=0)
        back_s = pltpu.roll(jnp.concatenate(part_s, axis=0), KA - 1, 1)
        d, g = dir_ref[m], grad_ref[m]
        product = d + amp * jnp.concatenate([back_c, back_s], axis=1)
        prod_ref[m] = product
        terms = (g * g, d * product, g * product, product * product)
        totals = [t + fold(x) for t, x in zip(totals, terms)]
    lane = lax.broadcasted_iota(i32, (1, 128), 1)
    line = jnp.zeros((1, 128), f32)
    for k, t in enumerate(totals):
        t = t + pltpu.roll(t, 64, 1)
        t = t + pltpu.roll(t, 32, 1)
        line = jnp.where((lane >> 5) == k, t, line)
    sums_ref[...] = line


def update(parts_ref, cont_ref, grad_ref, dir_ref, prod_ref, cont_out, grad_out, dir_out):
    line = jnp.sum(parts_ref[...], axis=0)
    group = lax.broadcasted_iota(i32, (1, 128), 1) >> 5
    grad_sq, curvature, cross, prod_sq = [
        jnp.sum(jnp.where(group == k, line, 0.0), axis=1, keepdims=True) for k in range(4)]
    step = grad_sq / curvature
    new_sq = grad_sq + step * (2.0 * cross + step * prod_sq)
    ratio = new_sq / grad_sq
    for m in range(LOCAL_M):
        d = dir_ref[m]
        fresh = grad_ref[m] + step * prod_ref[m]
        cont_out[m] = cont_ref[m] + step * d
        grad_out[m] = fresh
        dir_out[m] = ratio * d - fresh


def call(kernel, in_specs, outs, scratch=(), flops=0, moved=0, params=PARAMS):
    shapes = [jax.ShapeDtypeStruct(shape, dtype) for shape, dtype in outs]
    return pl.pallas_call(
        kernel,
        out_shape=shapes,
        in_specs=in_specs,
        out_specs=[VMEM] * len(shapes),
        scratch_shapes=list(scratch),
        compiler_params=params,
        cost_estimate=pl.CostEstimate(flops=flops, bytes_accessed=moved, transcendentals=0),
    )


def stage_to_rows(pencil, cutoff, direction):
    return call(
        to_rows, [SMEM, SMEM, HBM],
        [((N_SP, 1, CHUNK), f32), ((LOCAL_KB, 2 * KA), f32)],
        [pltpu.VMEM((8 * N_SP, 2 * KA), bf16), pltpu.VMEM((8 * N_SP, 2 * KA), bf16),
         pltpu.VMEM((LOCAL_M, LOCAL_KB, 2 * KA), f32), pltpu.SemaphoreType.DMA],
        flops=10 ** 8, moved=10 ** 6, params=WHOLE,
    )(pencil, cutoff, direction)


def stage_at_slots(count, index, weight, perturb):
    return call(
        at_slots, [SMEM] + [VMEM] * 3,
        [((2, 2 * KB, SLOTS), bf16), ((LOCAL_M, SLOTS), f32), ((1, SLOTS), f32)],
        flops=2 * 10 ** 9, moved=4 * 10 ** 6,
    )(count, index, weight, perturb)


def stage_sample(recv, basis, values, index):
    return call(
        sample, [VMEM] * 4, [((SLOTS // 128, 128), f32)], flops=3 * 10 ** 8, moved=2 * 10 ** 6,
    )(recv, basis, values, index)[0]


def stage_spread(parts, masked, basis, values, index):
    return call(
        spread, [VMEM] * 5, [((N_SP, 1, CHUNK), f32)], flops=3 * 10 ** 8, moved=2 * 10 ** 6,
    )(parts, masked, basis, values, index)[0]


def stage_from_rows(recv, phase, rows, amp, direction, gradient):
    return call(
        from_rows, [VMEM] * 6,
        [((LOCAL_M, LOCAL_KB, 2 * KA), f32), ((1, 128), f32)],
        flops=10 ** 8, moved=10 ** 6,
    )(recv, phase, rows, amp, direction, gradient)


def stage_update(parts, control, gradient, direction, product):
    shape = (LOCAL_M, LOCAL_KB, 2 * KA)
    return call(
        update, [VMEM] * 5, [(shape, f32)] * 3, flops=10 ** 5, moved=10 ** 5,
    )(parts, control, gradient, direction, product)


def swap(x):
    return lax.all_to_all(x, "sp", 0, 0, axis_index_groups=[ORDER], tiled=True)


def share(x, axis, count, groups=None):
    x = jnp.broadcast_to(x[None], (count,) + x.shape)
    return lax.all_to_all(x, axis, 0, 0, axis_index_groups=groups, tiled=True)


def shards(phase, rows, control, gradient, direction, perturb, obs_index, obs_count, obs_weight, cutoff):
    pencil = lax.axis_index("sp").astype(i32).reshape(1)
    send, amp = stage_to_rows(pencil, cutoff, direction)
    basis, values, masked = stage_at_slots(
        obs_count, obs_index, obs_weight, perturb.reshape(LOCAL_M * LEVELS * ROWS, NB))
    part = stage_sample(swap(send), basis, values, obs_index)
    send = stage_spread(share(part, "mem", SIDE), masked, basis, values, obs_index)
    product, sums = stage_from_rows(swap(send), phase, rows, amp, direction, gradient)
    sums = jnp.sum(share(sums, ("mem", "sp"), len(NEAR[0]), NEAR), axis=0)
    sums = share(sums, ("mem", "sp"), len(FAR[0]), FAR)
    return tuple(stage_update(sums, control, gradient, direction, product))


def solution(mesh):
    spectral = P("mem", "sp", None)
    placed = (spectral, spectral, spectral, P("mem", None, "sp", None), P("sp", None), P("sp"), P("sp", None), P())
    phase, rows = tables()
    return jax.shard_map(
        functools.partial(shards, phase, rows),
        mesh=mesh,
        in_specs=placed,
        out_specs=(spectral, spectral, spectral),
        check_vma=False,
    )
```

```python
import functools
import math

import jax
import jax.numpy as jnp
import numpy as np
from jax import lax
from jax.experimental import pallas as pl
from jax.experimental.pallas import tpu as pltpu
from jax.sharding import PartitionSpec as P

NA, NB, KA, KB = 3072, 1536, 256, 128
LEVELS, SLOTS, MEMBERS, ROWS, N_SP = 2, 2048, 16, 48, 64
LOCAL_M, LOCAL_KB = 2, 4
SIDE = 8
SCALE = 1.0 / math.sqrt(MEMBERS - 1)
CHUNK = LOCAL_KB * LOCAL_M * ROWS

f32, bf16, i32 = jnp.float32, jnp.bfloat16, jnp.int32
VMEM = pl.BlockSpec(memory_space=pltpu.VMEM)
HBM = pl.BlockSpec(memory_space=pltpu.HBM)
SMEM = pl.BlockSpec(memory_space=pltpu.SMEM)
PARAMS = pltpu.CompilerParams(vmem_limit_bytes=40 * 1024 * 1024)
WHOLE = pltpu.CompilerParams(vmem_limit_bytes=60 * 1024 * 1024)


def tables():
    w = np.arange(KA, dtype=np.int64)
    s = np.arange(N_SP, dtype=np.int64)[:, None]
    turn = 2.0 * np.pi * ((s * w) % N_SP) / N_SP
    r = np.arange(ROWS, dtype=np.int64)[:, None]
    ws = np.where(w == 0, KA, w)
    cos_rows = np.cos(2.0 * np.pi * ((r * w) % NA) / NA)
    sin_rows = np.sin(2.0 * np.pi * ((r * ws) % NA) / NA)
    rows = np.concatenate([cos_rows, sin_rows], axis=1).astype(np.float32)
    phase = np.stack([np.cos(turn), np.sin(turn)]).astype(np.float32)
    return phase, rows


def split(x):
    high = x.astype(bf16)
    return high, (x - high.astype(f32)).astype(bf16)


def dot(a, b, dims):
    return lax.dot_general(a, b, (dims, ((), ())), preferred_element_type=f32)


def wave(column, modes):
    return jnp.where(column < modes, column, column - modes + 1)


def shape_factor(radius, cutoff):
    retained = 4096 * radius <= cutoff * cutoff * (KA * KA)
    factor = 1.0 / (1.0 + (16.0 / (KA * KA)) * radius.astype(f32))
    return jnp.where(retained, factor, 0.0)


def to_rows(pen_ref, cut_ref, dir_in, out_ref, amp_ref, high_ref, low_ref, dir_ref, sem):
    dir_copy = pltpu.make_async_copy(dir_in, dir_ref, sem)
    dir_copy.start()
    w = lax.broadcasted_iota(i32, (1, KA), 1)
    s = lax.broadcasted_iota(i32, (N_SP, 1), 0)
    phase_c, phase_s = turns_to_cos_sin(((s * w) & (N_SP - 1)).astype(f32) * (1.0 / N_SP))
    r = lax.broadcasted_iota(i32, (ROWS, 1), 0)
    slot = lax.broadcasted_iota(i32, (1, 2 * KA), 1)
    ws = jnp.where(slot < KA, slot, jnp.where(slot == KA, KA, slot - KA))
    cos_r, sin_r = turns_to_cos_sin(residue_turns(ws.astype(f32), r.astype(f32), NA))
    table_high, table_low = split(jnp.where(slot < KA, cos_r, sin_r))
    cutoff, pencil = cut_ref[0], pen_ref[0]
    wa = lax.broadcasted_iota(i32, (1, 384), 1)
    wb = lax.broadcasted_iota(i32, (136, 1), 0)
    count_a = jnp.where(wa > KA, 0.0, jnp.where((wa == 0) | (wa == KA), 1.0, 2.0))
    count_b = jnp.where(wb > KB, 0.0, jnp.where((wb == 0) | (wb == KB), 1.0, 2.0))
    factor = shape_factor(wa * wa + 4 * (wb * wb), cutoff)
    energy = jnp.sum(factor * factor * count_a * count_b, axis=0, keepdims=True)
    energy = jnp.sum(energy, axis=1, keepdims=True)
    gain = jnp.sqrt(2.0 / energy)
    wa = wave(lax.broadcasted_iota(i32, (1, 2 * KA), 1), KA)
    wb = wave(lax.broadcasted_iota(i32, (LOCAL_KB, 1), 0) + pencil * LOCAL_KB, KB)
    amp = shape_factor(wa * wa + 4 * (wb * wb), cutoff) * gain
    amp_ref[...] = amp

    dir_copy.wait()
    for m in range(LOCAL_M):
        spectral = amp * dir_ref[m]
        part_c = spectral[:, :KA]
        part_s = pltpu.roll(spectral[:, KA:], 1, 1)
        for k in range(LOCAL_KB):
            c, s = part_c[k:k + 1], part_s[k:k + 1]
            at = pl.ds((k * LOCAL_M + m) * N_SP, N_SP)
            for half, value in ((0, c * phase_c + s * phase_s), (1, s * phase_c - c * phase_s)):
                high, low = split(value)
                high_ref[at, half * KA:(half + 1) * KA] = high
                low_ref[at, half * KA:(half + 1) * KA] = low
    nt = ((1,), (1,))
    result = (dot(high_ref[...], table_high, nt) + dot(high_ref[...], table_low, nt)
              + dot(low_ref[...], table_high, nt))
    pieces = [result[i * N_SP:(i + 1) * N_SP] for i in range(LOCAL_M * LOCAL_KB)]
    out_ref[:, 0, :] = jnp.concatenate(pieces, axis=1)


def cell_parts(index_ref):
    index = index_ref[...]
    line = jnp.floor((index.astype(f32) + 0.5) * (1.0 / NB)).astype(i32)
    column = index - line * NB
    return line, column


def turns_to_cos_sin(turns):
    quarter = jnp.floor(turns * 4.0 + 0.5)
    x = (turns - quarter * 0.25) * (2.0 * math.pi)
    x2 = x * x
    s = x * (1.0 + x2 * (-1.0 / 6 + x2 * (1.0 / 120 + x2 * (-1.0 / 5040 + x2 * (1.0 / 362880)))))
    c = 1.0 + x2 * (-0.5 + x2 * (1.0 / 24 + x2 * (-1.0 / 720 + x2 * (1.0 / 40320))))
    q = quarter.astype(i32) & 3
    odd = (q & 1) == 1
    cos = jnp.where(odd, s, c)
    sin = jnp.where(odd, c, s)
    return jnp.where((q == 1) | (q == 2), -cos, cos), jnp.where(q >= 2, -sin, sin)


def residue_turns(wavenum, place, length):
    product = wavenum * place
    return (product - jnp.floor(product * (1.0 / length)) * length) * (1.0 / length)


def at_slots(index_ref, pert_ref, basis_ref, values_ref):
    block = 256

    @pl.loop(0, SLOTS // block)
    def _(step):
        at = pl.ds(pl.multiple_of(step * block, block), block)
        index = index_ref[:, at]
        line = jnp.floor((index.astype(f32) + 0.5) * (1.0 / NB)).astype(i32)
        column = index - line * NB
        place = column.astype(f32)
        y = lax.broadcasted_iota(i32, (SIDE, 1), 0)
        cos_y, sin_y = turns_to_cos_sin(residue_turns((4 * y).astype(f32), place, NB))
        q = lax.broadcasted_iota(i32, (SIDE * LOCAL_KB, 1), 0)
        is_sin = (q & 7) >= SIDE // 2
        wq = (32 * (q & 3) + (q >> 3) + is_sin.astype(i32)).astype(f32)
        cos_q, sin_q = turns_to_cos_sin(residue_turns(wq, place, NB) - jnp.where(is_sin, 0.25, 0.0))
        for pair in range(SIDE * LOCAL_KB // 2):
            both = [cos_y * cos_q[g:g + 1] - sin_y * sin_q[g:g + 1] for g in (2 * pair, 2 * pair + 1)]
            high, low = split(jnp.concatenate(both, axis=0))
            basis_ref[0, pair * 16:(pair + 1) * 16, at] = high
            basis_ref[1, pair * 16:(pair + 1) * 16, at] = low
        lines = LEVELS * ROWS
        grid_column = lax.broadcasted_iota(i32, (NB, block), 0)
        chosen = jnp.where(grid_column == column, 1.0, 0.0).astype(bf16)
        found = dot(pert_ref[...], chosen, ((1,), (0,)))
        mine = lax.broadcasted_iota(i32, (lines, block), 0) == line
        for m in range(LOCAL_M):
            part = jnp.where(mine, found[m * lines:(m + 1) * lines], 0.0)
            values_ref[m:m + 1, at] = jnp.sum(part, axis=0, keepdims=True)


def sample(recv_ref, basis_ref, values_ref, index_ref, out_ref):
    wide = LOCAL_M * ROWS
    recv = recv_ref[:, 0, :]
    field = jnp.concatenate([recv[:, k * wide:(k + 1) * wide] for k in range(LOCAL_KB)], axis=0)
    high, low = split(field.T)
    nn = ((1,), (0,))
    both = dot(jnp.concatenate([high, low], axis=0), basis_ref[0], nn)
    rows = both[:wide] + both[wide:] + dot(high, basis_ref[1], nn)
    line, _ = cell_parts(index_ref)
    row = jnp.where(line >= ROWS, line - ROWS, line)
    mine = lax.broadcasted_iota(i32, (ROWS, SLOTS), 0) == row
    total = jnp.zeros((1, SLOTS), f32)
    for m in range(LOCAL_M):
        part = jnp.sum(jnp.where(mine, rows[m * ROWS:(m + 1) * ROWS], 0.0), axis=0, keepdims=True)
        total += values_ref[m:m + 1] * part
    out_ref[...] = jnp.concatenate([total[:, i * 128:(i + 1) * 128] for i in range(SLOTS // 128)], axis=0)


def spread(count_ref, parts_ref, weight_ref, basis_ref, values_ref, index_ref, out_ref):
    sampled = jnp.sum(parts_ref[...], axis=0)
    sampled = jnp.concatenate([sampled[i:i + 1] for i in range(SLOTS // 128)], axis=1)
    usable = lax.broadcasted_iota(i32, (1, SLOTS), 1) < count_ref[0]
    weighted = jnp.where(usable, (weight_ref[...] * (SCALE * SCALE)) * sampled, 0.0)
    line, _ = cell_parts(index_ref)
    row = jnp.where(line >= ROWS, line - ROWS, line)
    mine = lax.broadcasted_iota(i32, (ROWS, SLOTS), 0) == row
    highs, lows = [], []
    for m in range(LOCAL_M):
        value = values_ref[m:m + 1] * weighted
        high = value.astype(bf16).astype(f32)
        highs.append(jnp.where(mine, high, 0.0).astype(bf16))
        lows.append(jnp.where(mine, value - high, 0.0).astype(bf16))
    empty = jnp.zeros((32, SLOTS), bf16)
    right = jnp.concatenate(highs + [empty] + lows + [empty], axis=0)
    nt = ((1,), (1,))
    both = dot(basis_ref[0], right, nt)
    result = both[:, :128] + both[:, 128:] + dot(basis_ref[1], right[:128], nt)
    wide = LOCAL_M * ROWS
    pieces = [result[k * N_SP:(k + 1) * N_SP, :wide] for k in range(LOCAL_KB)]
    out_ref[:, 0, :] = jnp.concatenate(pieces, axis=1)


def fold(x):
    x = jnp.sum(x, axis=0, keepdims=True)
    return x[:, :128] + x[:, 128:256] + x[:, 256:384] + x[:, 384:]


def from_rows(recv_ref, phase_ref, rows_ref, amp_ref, dir_ref, grad_ref, prod_ref, sums_ref):
    count = LOCAL_M * LOCAL_KB
    recv = recv_ref[:, 0, :]
    left = jnp.concatenate([recv[:, i * ROWS:(i + 1) * ROWS] for i in range(count)], axis=0)
    high, low = split(left)
    nn = ((1,), (0,))
    table_high, table_low = split(rows_ref[...])
    turned = dot(high, table_high, nn) + dot(high, table_low, nn) + dot(low, table_high, nn)
    phase_c, phase_s = phase_ref[0], phase_ref[1]
    amp = amp_ref[...]
    totals = [jnp.zeros((1, 128), f32)] * 4
    for m in range(LOCAL_M):
        part_c, part_s = [], []
        for k in range(LOCAL_KB):
            i = k * LOCAL_M + m
            p, q = turned[i * N_SP:(i + 1) * N_SP, :KA], turned[i * N_SP:(i + 1) * N_SP, KA:]
            part_c.append(jnp.sum(p * phase_c - q * phase_s, axis=0, keepdims=True))
            part_s.append(jnp.sum(p * phase_s + q * phase_c, axis=0, keepdims=True))
        back_c = jnp.concatenate(part_c, axis=0)
        back_s = pltpu.roll(jnp.concatenate(part_s, axis=0), KA - 1, 1)
        d, g = dir_ref[m], grad_ref[m]
        product = d + amp * jnp.concatenate([back_c, back_s], axis=1)
        prod_ref[m] = product
        terms = (g * g, d * product, g * product, product * product)
        totals = [t + fold(x) for t, x in zip(totals, terms)]
    lane = lax.broadcasted_iota(i32, (1, 128), 1)
    line = jnp.zeros((1, 128), f32)
    for k, t in enumerate(totals):
        t = t + pltpu.roll(t, 64, 1)
        t = t + pltpu.roll(t, 32, 1)
        line = jnp.where((lane >> 5) == k, t, line)
    sums_ref[...] = line


def update(parts_ref, cont_ref, grad_ref, dir_ref, prod_ref, cont_out, grad_out, dir_out):
    line = jnp.sum(parts_ref[...], axis=0)
    group = lax.broadcasted_iota(i32, (1, 128), 1) >> 5
    grad_sq, curvature, cross, prod_sq = [
        jnp.sum(jnp.where(group == k, line, 0.0), axis=1, keepdims=True) for k in range(4)]
    step = grad_sq / curvature
    new_sq = grad_sq + step * (2.0 * cross + step * prod_sq)
    ratio = new_sq / grad_sq
    for m in range(LOCAL_M):
        d = dir_ref[m]
        fresh = grad_ref[m] + step * prod_ref[m]
        cont_out[m] = cont_ref[m] + step * d
        grad_out[m] = fresh
        dir_out[m] = ratio * d - fresh


def call(kernel, in_specs, outs, scratch=(), flops=0, moved=0, params=PARAMS):
    shapes = [jax.ShapeDtypeStruct(shape, dtype) for shape, dtype in outs]
    return pl.pallas_call(
        kernel,
        out_shape=shapes,
        in_specs=in_specs,
        out_specs=[VMEM] * len(shapes),
        scratch_shapes=list(scratch),
        compiler_params=params,
        cost_estimate=pl.CostEstimate(flops=flops, bytes_accessed=moved, transcendentals=0),
    )


def stage_to_rows(pencil, cutoff, direction):
    return call(
        to_rows, [SMEM, SMEM, HBM],
        [((N_SP, 1, CHUNK), f32), ((LOCAL_KB, 2 * KA), f32)],
        [pltpu.VMEM((8 * N_SP, 2 * KA), bf16), pltpu.VMEM((8 * N_SP, 2 * KA), bf16),
         pltpu.VMEM((LOCAL_M, LOCAL_KB, 2 * KA), f32), pltpu.SemaphoreType.DMA],
        flops=10 ** 8, moved=10 ** 6, params=WHOLE,
    )(pencil, cutoff, direction)


def stage_at_slots(index, perturb):
    return call(
        at_slots, [VMEM] * 2,
        [((2, 2 * KB, SLOTS), bf16), ((LOCAL_M, SLOTS), f32)],
        flops=2 * 10 ** 9, moved=4 * 10 ** 6,
    )(index, perturb)


def stage_sample(recv, basis, values, index):
    return call(
        sample, [VMEM] * 4, [((SLOTS // 128, 128), f32)], flops=3 * 10 ** 8, moved=2 * 10 ** 6,
    )(recv, basis, values, index)[0]


def stage_spread(count, parts, weight, basis, values, index):
    return call(
        spread, [SMEM] + [VMEM] * 5, [((N_SP, 1, CHUNK), f32)], flops=3 * 10 ** 8, moved=2 * 10 ** 6,
    )(count, parts, weight, basis, values, index)[0]


def stage_from_rows(recv, phase, rows, amp, direction, gradient):
    return call(
        from_rows, [VMEM] * 6,
        [((LOCAL_M, LOCAL_KB, 2 * KA), f32), ((1, 128), f32)],
        flops=10 ** 8, moved=10 ** 6,
    )(recv, phase, rows, amp, direction, gradient)


def stage_update(parts, control, gradient, direction, product):
    shape = (LOCAL_M, LOCAL_KB, 2 * KA)
    return call(
        update, [VMEM] * 5, [(shape, f32)] * 3, flops=10 ** 5, moved=10 ** 5,
    )(parts, control, gradient, direction, product)


NEAR = [[m * N_SP + s + y for m in range(SIDE) for y in range(2)] for s in range(0, N_SP, 2)]
FAR = [[m * N_SP + s + y for s in range(0, N_SP, 2)] for m in range(SIDE) for y in range(2)]


def swap(x):
    return lax.all_to_all(x, "sp", 0, 0, tiled=True)


def share(x, axis, count, groups=None):
    x = jnp.broadcast_to(x[None], (count,) + x.shape)
    return lax.all_to_all(x, axis, 0, 0, axis_index_groups=groups, tiled=True)


def shards(phase, rows, control, gradient, direction, perturb, obs_index, obs_count, obs_weight, cutoff):
    pencil = lax.axis_index("sp").astype(i32).reshape(1)
    send, amp = stage_to_rows(pencil, cutoff, direction)
    basis, values = stage_at_slots(obs_index, perturb.reshape(LOCAL_M * LEVELS * ROWS, NB))
    part = stage_sample(swap(send), basis, values, obs_index)
    send = stage_spread(obs_count, share(part, "mem", SIDE), obs_weight, basis, values, obs_index)
    product, sums = stage_from_rows(swap(send), phase, rows, amp, direction, gradient)
    sums = jnp.sum(share(sums, ("mem", "sp"), len(NEAR[0]), NEAR), axis=0)
    sums = share(sums, ("mem", "sp"), len(FAR[0]), FAR)
    return tuple(stage_update(sums, control, gradient, direction, product))


def solution(mesh):
    spectral = P("mem", "sp", None)
    placed = (spectral, spectral, spectral, P("mem", None, "sp", None), P("sp", None), P("sp"), P("sp", None), P())
    phase, rows = tables()
    return jax.shard_map(
        functools.partial(shards, phase, rows),
        mesh=mesh,
        in_specs=placed,
        out_specs=(spectral, spectral, spectral),
        check_vma=False,
    )
```

```python
import functools
import math

import jax
import jax.numpy as jnp
import numpy as np
from jax import lax
from jax.experimental import pallas as pl
from jax.experimental.pallas import tpu as pltpu
from jax.sharding import PartitionSpec as P

NA, NB, KA, KB = 3072, 1536, 256, 128
LEVELS, SLOTS, MEMBERS, ROWS, N_SP = 2, 2048, 16, 48, 64
LOCAL_M, LOCAL_KB = 2, 4
SIDE = 8
SCALE = 1.0 / math.sqrt(MEMBERS - 1)
CHUNK = LOCAL_KB * LOCAL_M * ROWS

f32, bf16, i32 = jnp.float32, jnp.bfloat16, jnp.int32
VMEM = pl.BlockSpec(memory_space=pltpu.VMEM)
HBM = pl.BlockSpec(memory_space=pltpu.HBM)
SMEM = pl.BlockSpec(memory_space=pltpu.SMEM)
PARAMS = pltpu.CompilerParams(vmem_limit_bytes=40 * 1024 * 1024)
WHOLE = pltpu.CompilerParams(vmem_limit_bytes=60 * 1024 * 1024)


def tables():
    w = np.arange(KA, dtype=np.int64)
    s = np.arange(N_SP, dtype=np.int64)[:, None]
    turn = 2.0 * np.pi * ((s * w) % N_SP) / N_SP
    r = np.arange(ROWS, dtype=np.int64)[:, None]
    ws = np.where(w == 0, KA, w)
    cos_rows = np.cos(2.0 * np.pi * ((r * w) % NA) / NA)
    sin_rows = np.sin(2.0 * np.pi * ((r * ws) % NA) / NA)
    rows = np.concatenate([cos_rows, sin_rows], axis=1).astype(np.float32)
    phase = np.stack([np.cos(turn), np.sin(turn)]).astype(np.float32)
    return phase, rows


def split(x):
    high = x.astype(bf16)
    return high, (x - high.astype(f32)).astype(bf16)


def dot(a, b, dims):
    return lax.dot_general(a, b, (dims, ((), ())), preferred_element_type=f32)


def wave(column, modes):
    return jnp.where(column < modes, column, column - modes + 1)


def shape_factor(radius, cutoff):
    retained = 4096 * radius <= cutoff * cutoff * (KA * KA)
    factor = 1.0 / (1.0 + (16.0 / (KA * KA)) * radius.astype(f32))
    return jnp.where(retained, factor, 0.0)


def to_rows(pen_ref, cut_ref, dir_in, out_ref, amp_ref, high_ref, low_ref, dir_ref, sem):
    dir_copy = pltpu.make_async_copy(dir_in, dir_ref, sem)
    dir_copy.start()
    w = lax.broadcasted_iota(i32, (1, 128), 1)
    s = lax.broadcasted_iota(i32, (N_SP, 1), 0)
    phase_c, phase_s = turns_to_cos_sin(((s * w) & (N_SP - 1)).astype(f32) * (1.0 / N_SP))
    phase_c = jnp.concatenate([phase_c, phase_c], axis=1)
    phase_s = jnp.concatenate([phase_s, phase_s], axis=1)
    r = lax.broadcasted_iota(i32, (ROWS, 1), 0)
    w = lax.broadcasted_iota(i32, (1, KA), 1)
    ws = jnp.where(w == 0, KA, w)
    cos_r, sin_r = turns_to_cos_sin(residue_turns(ws.astype(f32), r.astype(f32), NA))
    table_high, table_low = split(jnp.concatenate([jnp.where(w == 0, 1.0, cos_r), sin_r], axis=1))
    cutoff, pencil = cut_ref[0], pen_ref[0]
    wa = lax.broadcasted_iota(i32, (1, 384), 1)
    wb = lax.broadcasted_iota(i32, (136, 1), 0)
    count_a = jnp.where(wa > KA, 0.0, jnp.where((wa == 0) | (wa == KA), 1.0, 2.0))
    count_b = jnp.where(wb > KB, 0.0, jnp.where((wb == 0) | (wb == KB), 1.0, 2.0))
    factor = shape_factor(wa * wa + 4 * (wb * wb), cutoff)
    energy = jnp.sum(factor * factor * count_a * count_b, axis=0, keepdims=True)
    energy = jnp.sum(energy, axis=1, keepdims=True)
    gain = jnp.sqrt(2.0 / energy)
    wa = wave(lax.broadcasted_iota(i32, (1, 2 * KA), 1), KA)
    wb = wave(lax.broadcasted_iota(i32, (LOCAL_KB, 1), 0) + pencil * LOCAL_KB, KB)
    amp = shape_factor(wa * wa + 4 * (wb * wb), cutoff) * gain
    amp_ref[...] = amp

    dir_copy.wait()
    for m in range(LOCAL_M):
        spectral = amp * dir_ref[m]
        part_c = spectral[:, :KA]
        part_s = pltpu.roll(spectral[:, KA:], 1, 1)
        for k in range(LOCAL_KB):
            c, s = part_c[k:k + 1], part_s[k:k + 1]
            at = pl.ds((k * LOCAL_M + m) * N_SP, N_SP)
            for half, value in ((0, c * phase_c + s * phase_s), (1, s * phase_c - c * phase_s)):
                high, low = split(value)
                high_ref[at, half * KA:(half + 1) * KA] = high
                low_ref[at, half * KA:(half + 1) * KA] = low
    nt = ((1,), (1,))
    result = (dot(high_ref[...], table_high, nt) + dot(high_ref[...], table_low, nt)
              + dot(low_ref[...], table_high, nt))
    pieces = [result[i * N_SP:(i + 1) * N_SP] for i in range(LOCAL_M * LOCAL_KB)]
    out_ref[:, 0, :] = jnp.concatenate(pieces, axis=1)


def cell_parts(index_ref):
    index = index_ref[...]
    line = jnp.floor((index.astype(f32) + 0.5) * (1.0 / NB)).astype(i32)
    column = index - line * NB
    return line, column


def turns_to_cos_sin(turns):
    quarter = jnp.floor(turns * 4.0 + 0.5)
    x = (turns - quarter * 0.25) * (2.0 * math.pi)
    x2 = x * x
    s = x * (1.0 + x2 * (-1.0 / 6 + x2 * (1.0 / 120 + x2 * (-1.0 / 5040 + x2 * (1.0 / 362880)))))
    c = 1.0 + x2 * (-0.5 + x2 * (1.0 / 24 + x2 * (-1.0 / 720 + x2 * (1.0 / 40320))))
    q = quarter.astype(i32) & 3
    odd = (q & 1) == 1
    cos = jnp.where(odd, s, c)
    sin = jnp.where(odd, c, s)
    return jnp.where((q == 1) | (q == 2), -cos, cos), jnp.where(q >= 2, -sin, sin)


def residue_turns(wavenum, place, length):
    product = wavenum * place
    return (product - jnp.floor(product * (1.0 / length)) * length) * (1.0 / length)


def at_slots(index_ref, pert_ref, basis_ref, values_ref):
    block = 256

    @pl.loop(0, SLOTS // block)
    def _(step):
        at = pl.ds(pl.multiple_of(step * block, block), block)
        index = index_ref[:, at]
        line = jnp.floor((index.astype(f32) + 0.5) * (1.0 / NB)).astype(i32)
        column = index - line * NB
        place = column.astype(f32)
        y = lax.broadcasted_iota(i32, (SIDE, 1), 0)
        cos_y, sin_y = turns_to_cos_sin(residue_turns((4 * y).astype(f32), place, NB))
        q = lax.broadcasted_iota(i32, (SIDE * LOCAL_KB, 1), 0)
        is_sin = (q & 7) >= SIDE // 2
        wq = (32 * (q & 3) + (q >> 3) + is_sin.astype(i32)).astype(f32)
        cos_q, sin_q = turns_to_cos_sin(residue_turns(wq, place, NB) - jnp.where(is_sin, 0.25, 0.0))
        for pair in range(SIDE * LOCAL_KB // 2):
            both = [cos_y * cos_q[g:g + 1] - sin_y * sin_q[g:g + 1] for g in (2 * pair, 2 * pair + 1)]
            high, low = split(jnp.concatenate(both, axis=0))
            basis_ref[0, pair * 16:(pair + 1) * 16, at] = high
            basis_ref[1, pair * 16:(pair + 1) * 16, at] = low
        lines = LEVELS * ROWS
        grid_column = lax.broadcasted_iota(i32, (NB, block), 0)
        chosen = jnp.where(grid_column == column, 1.0, 0.0).astype(bf16)
        found = dot(pert_ref[...], chosen, ((1,), (0,)))
        mine = lax.broadcasted_iota(i32, (lines, block), 0) == line
        for m in range(LOCAL_M):
            part = jnp.where(mine, found[m * lines:(m + 1) * lines], 0.0)
            values_ref[m:m + 1, at] = jnp.sum(part, axis=0, keepdims=True)


def sample(recv_ref, basis_ref, values_ref, index_ref, out_ref):
    wide = LOCAL_M * ROWS
    recv = recv_ref[:, 0, :]
    field = jnp.concatenate([recv[:, k * wide:(k + 1) * wide] for k in range(LOCAL_KB)], axis=0)
    high, low = split(field.T)
    nn = ((1,), (0,))
    both = dot(jnp.concatenate([high, low], axis=0), basis_ref[0], nn)
    rows = both[:wide] + both[wide:] + dot(high, basis_ref[1], nn)
    line, _ = cell_parts(index_ref)
    row = jnp.where(line >= ROWS, line - ROWS, line)
    mine = lax.broadcasted_iota(i32, (ROWS, SLOTS), 0) == row
    total = jnp.zeros((1, SLOTS), f32)
    for m in range(LOCAL_M):
        part = jnp.sum(jnp.where(mine, rows[m * ROWS:(m + 1) * ROWS], 0.0), axis=0, keepdims=True)
        total += values_ref[m:m + 1] * part
    dense = jnp.concatenate([total[:, i * 128:(i + 1) * 128] for i in range(SLOTS // 128)], axis=0)
    for i in range(SIDE):
        out_ref[i] = dense


def spread(count_ref, parts_ref, weight_ref, basis_ref, values_ref, index_ref, out_ref):
    sampled = jnp.sum(parts_ref[...], axis=0)
    sampled = jnp.concatenate([sampled[i:i + 1] for i in range(SLOTS // 128)], axis=1)
    usable = lax.broadcasted_iota(i32, (1, SLOTS), 1) < count_ref[0]
    weighted = jnp.where(usable, (weight_ref[...] * (SCALE * SCALE)) * sampled, 0.0)
    line, _ = cell_parts(index_ref)
    row = jnp.where(line >= ROWS, line - ROWS, line)
    mine = lax.broadcasted_iota(i32, (ROWS, SLOTS), 0) == row
    highs, lows = [], []
    for m in range(LOCAL_M):
        value = values_ref[m:m + 1] * weighted
        high = value.astype(bf16).astype(f32)
        highs.append(jnp.where(mine, high, 0.0).astype(bf16))
        lows.append(jnp.where(mine, value - high, 0.0).astype(bf16))
    empty = jnp.zeros((32, SLOTS), bf16)
    right = jnp.concatenate(highs + [empty] + lows + [empty], axis=0)
    nt = ((1,), (1,))
    both = dot(basis_ref[0], right, nt)
    result = both[:, :128] + both[:, 128:] + dot(basis_ref[1], right[:128], nt)
    wide = LOCAL_M * ROWS
    pieces = [result[k * N_SP:(k + 1) * N_SP, :wide] for k in range(LOCAL_KB)]
    out_ref[:, 0, :] = jnp.concatenate(pieces, axis=1)


def fold(x):
    x = jnp.sum(x, axis=0, keepdims=True)
    return x[:, :128] + x[:, 128:256] + x[:, 256:384] + x[:, 384:]


def from_rows(recv_ref, phase_ref, rows_ref, amp_ref, dir_ref, grad_ref, square_ref, prod_ref, sums_ref):
    count = LOCAL_M * LOCAL_KB
    recv = recv_ref[:, 0, :]
    left = jnp.concatenate([recv[:, i * ROWS:(i + 1) * ROWS] for i in range(count)], axis=0)
    high, low = split(left)
    nn = ((1,), (0,))
    table_high, table_low = split(rows_ref[...])
    turned = dot(high, table_high, nn) + dot(high, table_low, nn) + dot(low, table_high, nn)
    phase_c, phase_s = phase_ref[0], phase_ref[1]
    amp = amp_ref[...]
    totals = [jnp.zeros((1, 128), f32)] * 3
    for m in range(LOCAL_M):
        part_c, part_s = [], []
        for k in range(LOCAL_KB):
            i = k * LOCAL_M + m
            p, q = turned[i * N_SP:(i + 1) * N_SP, :KA], turned[i * N_SP:(i + 1) * N_SP, KA:]
            part_c.append(jnp.sum(p * phase_c - q * phase_s, axis=0, keepdims=True))
            part_s.append(jnp.sum(p * phase_s + q * phase_c, axis=0, keepdims=True))
        back_c = jnp.concatenate(part_c, axis=0)
        back_s = pltpu.roll(jnp.concatenate(part_s, axis=0), KA - 1, 1)
        d, g = dir_ref[m], grad_ref[m]
        product = d + amp * jnp.concatenate([back_c, back_s], axis=1)
        prod_ref[m] = product
        terms = (d * product, g * product, product * product)
        totals = [t + fold(x) for t, x in zip(totals, terms)]
    lane = lax.broadcasted_iota(i32, (1, 128), 1)
    line = jnp.zeros((1, 128), f32)
    for k, t in enumerate([fold(square_ref[...])] + totals):
        t = t + pltpu.roll(t, 64, 1)
        t = t + pltpu.roll(t, 32, 1)
        line = jnp.where((lane >> 5) == k, t, line)
    sums_ref[...] = line


def update(parts_ref, cont_ref, grad_ref, dir_ref, prod_ref, cont_out, grad_out, dir_out):
    line = jnp.sum(parts_ref[...], axis=0)
    group = lax.broadcasted_iota(i32, (1, 128), 1) >> 5
    grad_sq, curvature, cross, prod_sq = [
        jnp.sum(jnp.where(group == k, line, 0.0), axis=1, keepdims=True) for k in range(4)]
    step = grad_sq / curvature
    new_sq = grad_sq + step * (2.0 * cross + step * prod_sq)
    ratio = new_sq / grad_sq
    for m in range(LOCAL_M):
        d = dir_ref[m]
        fresh = grad_ref[m] + step * prod_ref[m]
        cont_out[m] = cont_ref[m] + step * d
        grad_out[m] = fresh
        dir_out[m] = ratio * d - fresh


def call(kernel, in_specs, outs, scratch=(), flops=0, moved=0, params=PARAMS):
    shapes = [jax.ShapeDtypeStruct(shape, dtype) for shape, dtype in outs]
    return pl.pallas_call(
        kernel,
        out_shape=shapes,
        in_specs=in_specs,
        out_specs=[VMEM] * len(shapes),
        scratch_shapes=list(scratch),
        compiler_params=params,
        cost_estimate=pl.CostEstimate(flops=flops, bytes_accessed=moved, transcendentals=0),
    )


def stage_to_rows(pencil, cutoff, direction):
    return call(
        to_rows, [SMEM, SMEM, HBM],
        [((N_SP, 1, CHUNK), f32), ((LOCAL_KB, 2 * KA), f32)],
        [pltpu.VMEM((8 * N_SP, 2 * KA), bf16), pltpu.VMEM((8 * N_SP, 2 * KA), bf16),
         pltpu.VMEM((LOCAL_M, LOCAL_KB, 2 * KA), f32), pltpu.SemaphoreType.DMA],
        flops=10 ** 8, moved=10 ** 6, params=WHOLE,
    )(pencil, cutoff, direction)


def stage_at_slots(index, perturb):
    return call(
        at_slots, [VMEM] * 2,
        [((2, 2 * KB, SLOTS), bf16), ((LOCAL_M, SLOTS), f32)],
        flops=2 * 10 ** 9, moved=4 * 10 ** 6,
    )(index, perturb)


def stage_sample(recv, basis, values, index):
    return call(
        sample, [VMEM] * 4, [((SIDE, SLOTS // 128, 128), f32)], flops=3 * 10 ** 8, moved=2 * 10 ** 6,
    )(recv, basis, values, index)[0]


def stage_spread(count, parts, weight, basis, values, index):
    return call(
        spread, [SMEM] + [VMEM] * 5, [((N_SP, 1, CHUNK), f32)], flops=3 * 10 ** 8, moved=2 * 10 ** 6,
    )(count, parts, weight, basis, values, index)[0]


def stage_from_rows(recv, phase, rows, amp, direction, gradient, square):
    return call(
        from_rows, [VMEM] * 7,
        [((LOCAL_M, LOCAL_KB, 2 * KA), f32), ((1, 128), f32)],
        flops=10 ** 8, moved=10 ** 6,
    )(recv, phase, rows, amp, direction, gradient, square)


def stage_update(parts, control, gradient, direction, product):
    shape = (LOCAL_M, LOCAL_KB, 2 * KA)
    return call(
        update, [VMEM] * 5, [(shape, f32)] * 3, flops=10 ** 5, moved=10 ** 5,
    )(parts, control, gradient, direction, product)


NEAR = [[m * N_SP + s + y for m in range(SIDE) for y in range(2)] for s in range(0, N_SP, 2)]
FAR = [[m * N_SP + s + y for s in range(0, N_SP, 2)] for m in range(SIDE) for y in range(2)]


def swap(x):
    return lax.all_to_all(x, "sp", 0, 0, tiled=True)


def share(x, axis, count, groups=None):
    x = jnp.broadcast_to(x[None], (count,) + x.shape)
    return lax.all_to_all(x, axis, 0, 0, axis_index_groups=groups, tiled=True)


def shards(phase, rows, control, gradient, direction, perturb, obs_index, obs_count, obs_weight, cutoff):
    pencil = lax.axis_index("sp").astype(i32).reshape(1)
    send, amp = stage_to_rows(pencil, cutoff, direction)
    basis, values = stage_at_slots(obs_index, perturb.reshape(LOCAL_M * LEVELS * ROWS, NB))
    parts = lax.all_to_all(stage_sample(swap(send), basis, values, obs_index), "mem", 0, 0, tiled=True)
    send = stage_spread(obs_count, parts, obs_weight, basis, values, obs_index)
    square = jnp.sum(gradient * gradient, axis=(0, 1))[None]
    product, sums = stage_from_rows(swap(send), phase, rows, amp, direction, gradient, square)
    sums = jnp.sum(share(sums, ("mem", "sp"), len(NEAR[0]), NEAR), axis=0)
    sums = share(sums, ("mem", "sp"), len(FAR[0]), FAR)
    return tuple(stage_update(sums, control, gradient, direction, product))


def solution(mesh):
    spectral = P("mem", "sp", None)
    placed = (spectral, spectral, spectral, P("mem", None, "sp", None), P("sp", None), P("sp"), P("sp", None), P())
    phase, rows = tables()
    return jax.shard_map(
        functools.partial(shards, phase, rows),
        mesh=mesh,
        in_specs=placed,
        out_specs=(spectral, spectral, spectral),
        check_vma=False,
    )
```

```python
import functools
import math

import jax
import jax.numpy as jnp
import numpy as np
from jax import lax
from jax.experimental import pallas as pl
from jax.experimental.pallas import tpu as pltpu
from jax.sharding import PartitionSpec as P

NA, NB, KA, KB = 3072, 1536, 256, 128
LEVELS, SLOTS, MEMBERS, ROWS, N_SP = 2, 2048, 16, 48, 64
LOCAL_M, LOCAL_KB = 2, 4
SIDE = 8
SCALE = 1.0 / math.sqrt(MEMBERS - 1)
CHUNK = LOCAL_KB * LOCAL_M * ROWS

f32, bf16, i32 = jnp.float32, jnp.bfloat16, jnp.int32
VMEM = pl.BlockSpec(memory_space=pltpu.VMEM)
HBM = pl.BlockSpec(memory_space=pltpu.HBM)
SMEM = pl.BlockSpec(memory_space=pltpu.SMEM)
PARAMS = pltpu.CompilerParams(vmem_limit_bytes=40 * 1024 * 1024)
WHOLE = pltpu.CompilerParams(vmem_limit_bytes=60 * 1024 * 1024)


def tables():
    w = np.arange(KA, dtype=np.int64)
    s = np.arange(N_SP, dtype=np.int64)[:, None]
    turn = 2.0 * np.pi * ((s * w) % N_SP) / N_SP
    r = np.arange(ROWS, dtype=np.int64)[:, None]
    ws = np.where(w == 0, KA, w)
    cos_rows = np.cos(2.0 * np.pi * ((r * w) % NA) / NA)
    sin_rows = np.sin(2.0 * np.pi * ((r * ws) % NA) / NA)
    rows = np.concatenate([cos_rows, sin_rows], axis=1).astype(np.float32)
    phase = np.stack([np.cos(turn), np.sin(turn)]).astype(np.float32)
    return phase, rows


def split(x):
    high = x.astype(bf16)
    return high, (x - high.astype(f32)).astype(bf16)


def dot(a, b, dims):
    return lax.dot_general(a, b, (dims, ((), ())), preferred_element_type=f32)


def wave(column, modes):
    return jnp.where(column < modes, column, column - modes + 1)


def shape_factor(radius, cutoff):
    retained = 4096 * radius <= cutoff * cutoff * (KA * KA)
    factor = 1.0 / (1.0 + (16.0 / (KA * KA)) * radius.astype(f32))
    return jnp.where(retained, factor, 0.0)


def to_rows(pen_ref, cut_ref, dir_in, out_ref, amp_ref, high_ref, low_ref, dir_ref, sem):
    dir_copy = pltpu.make_async_copy(dir_in, dir_ref, sem)
    dir_copy.start()
    w = lax.broadcasted_iota(i32, (1, 128), 1)
    s = lax.broadcasted_iota(i32, (N_SP, 1), 0)
    phase_c, phase_s = turns_to_cos_sin(((s * w) & (N_SP - 1)).astype(f32) * (1.0 / N_SP))
    phase_c = jnp.concatenate([phase_c, phase_c], axis=1)
    phase_s = jnp.concatenate([phase_s, phase_s], axis=1)
    r = lax.broadcasted_iota(i32, (ROWS, 1), 0)
    w = lax.broadcasted_iota(i32, (1, KA), 1)
    ws = jnp.where(w == 0, KA, w)
    cos_r, sin_r = turns_to_cos_sin(residue_turns(ws.astype(f32), r.astype(f32), NA))
    table_high, table_low = split(jnp.concatenate([jnp.where(w == 0, 1.0, cos_r), sin_r], axis=1))
    cutoff, pencil = cut_ref[0], pen_ref[0]
    wa = lax.broadcasted_iota(i32, (1, 384), 1)
    wb = lax.broadcasted_iota(i32, (136, 1), 0)
    count_a = jnp.where(wa > KA, 0.0, jnp.where((wa == 0) | (wa == KA), 1.0, 2.0))
    count_b = jnp.where(wb > KB, 0.0, jnp.where((wb == 0) | (wb == KB), 1.0, 2.0))
    factor = shape_factor(wa * wa + 4 * (wb * wb), cutoff)
    energy = jnp.sum(factor * factor * count_a * count_b, axis=0, keepdims=True)
    energy = jnp.sum(energy, axis=1, keepdims=True)
    gain = jnp.sqrt(2.0 / energy)
    wa = wave(lax.broadcasted_iota(i32, (1, 2 * KA), 1), KA)
    wb = wave(lax.broadcasted_iota(i32, (LOCAL_KB, 1), 0) + pencil * LOCAL_KB, KB)
    amp = shape_factor(wa * wa + 4 * (wb * wb), cutoff) * gain
    amp_ref[...] = amp

    dir_copy.wait()
    nt = ((1,), (1,))
    pieces = [None] * (LOCAL_M * LOCAL_KB)
    for m in range(LOCAL_M):
        spectral = amp * dir_ref[m]
        part_c = spectral[:, :KA]
        part_s = pltpu.roll(spectral[:, KA:], 1, 1)
        for k in range(LOCAL_KB):
            c, s = part_c[k:k + 1], part_s[k:k + 1]
            at = pl.ds((m * LOCAL_KB + k) * N_SP, N_SP)
            for half, value in ((0, c * phase_c + s * phase_s), (1, s * phase_c - c * phase_s)):
                high, low = split(value)
                high_ref[at, half * KA:(half + 1) * KA] = high
                low_ref[at, half * KA:(half + 1) * KA] = low
        of_m = pl.ds(m * LOCAL_KB * N_SP, LOCAL_KB * N_SP)
        result = (dot(high_ref[of_m], table_high, nt) + dot(high_ref[of_m], table_low, nt)
                  + dot(low_ref[of_m], table_high, nt))
        for k in range(LOCAL_KB):
            pieces[k * LOCAL_M + m] = result[k * N_SP:(k + 1) * N_SP]
    out_ref[:, 0, :] = jnp.concatenate(pieces, axis=1)


def cell_parts(index_ref):
    index = index_ref[...]
    line = jnp.floor((index.astype(f32) + 0.5) * (1.0 / NB)).astype(i32)
    column = index - line * NB
    return line, column


def turns_to_cos_sin(turns):
    quarter = jnp.floor(turns * 4.0 + 0.5)
    x = (turns - quarter * 0.25) * (2.0 * math.pi)
    x2 = x * x
    s = x * (1.0 + x2 * (-1.0 / 6 + x2 * (1.0 / 120 + x2 * (-1.0 / 5040 + x2 * (1.0 / 362880)))))
    c = 1.0 + x2 * (-0.5 + x2 * (1.0 / 24 + x2 * (-1.0 / 720 + x2 * (1.0 / 40320))))
    q = quarter.astype(i32) & 3
    odd = (q & 1) == 1
    cos = jnp.where(odd, s, c)
    sin = jnp.where(odd, c, s)
    return jnp.where((q == 1) | (q == 2), -cos, cos), jnp.where(q >= 2, -sin, sin)


def residue_turns(wavenum, place, length):
    product = wavenum * place
    return (product - jnp.floor(product * (1.0 / length)) * length) * (1.0 / length)


def at_slots(index_ref, pert_ref, basis_ref, values_ref):
    block = 256

    @pl.loop(0, SLOTS // block)
    def _(step):
        at = pl.ds(pl.multiple_of(step * block, block), block)
        index = index_ref[:, at]
        line = jnp.floor((index.astype(f32) + 0.5) * (1.0 / NB)).astype(i32)
        column = index - line * NB
        place = column.astype(f32)
        y = lax.broadcasted_iota(i32, (SIDE, 1), 0)
        cos_y, sin_y = turns_to_cos_sin(residue_turns((4 * y).astype(f32), place, NB))
        q = lax.broadcasted_iota(i32, (SIDE * LOCAL_KB, 1), 0)
        is_sin = (q & 7) >= SIDE // 2
        wq = (32 * (q & 3) + (q >> 3) + is_sin.astype(i32)).astype(f32)
        cos_q, sin_q = turns_to_cos_sin(residue_turns(wq, place, NB) - jnp.where(is_sin, 0.25, 0.0))
        for pair in range(SIDE * LOCAL_KB // 2):
            both = [cos_y * cos_q[g:g + 1] - sin_y * sin_q[g:g + 1] for g in (2 * pair, 2 * pair + 1)]
            high, low = split(jnp.concatenate(both, axis=0))
            basis_ref[0, pair * 16:(pair + 1) * 16, at] = high
            basis_ref[1, pair * 16:(pair + 1) * 16, at] = low
        lines = LEVELS * ROWS
        grid_column = lax.broadcasted_iota(i32, (NB, block), 0)
        chosen = jnp.where(grid_column == column, 1.0, 0.0).astype(bf16)
        found = dot(pert_ref[...], chosen, ((1,), (0,)))
        mine = lax.broadcasted_iota(i32, (lines, block), 0) == line
        for m in range(LOCAL_M):
            part = jnp.where(mine, found[m * lines:(m + 1) * lines], 0.0)
            values_ref[m:m + 1, at] = jnp.sum(part, axis=0, keepdims=True)


def sample(recv_ref, basis_ref, values_ref, index_ref, out_ref):
    wide = LOCAL_M * ROWS
    recv = recv_ref[:, 0, :]
    field = jnp.concatenate([recv[:, k * wide:(k + 1) * wide] for k in range(LOCAL_KB)], axis=0)
    high, low = split(field.T)
    nn = ((1,), (0,))
    both = dot(jnp.concatenate([high, low], axis=0), basis_ref[0], nn)
    rows = both[:wide] + both[wide:] + dot(high, basis_ref[1], nn)
    line, _ = cell_parts(index_ref)
    row = jnp.where(line >= ROWS, line - ROWS, line)
    mine = lax.broadcasted_iota(i32, (ROWS, SLOTS), 0) == row
    total = jnp.zeros((1, SLOTS), f32)
    for m in range(LOCAL_M):
        part = jnp.sum(jnp.where(mine, rows[m * ROWS:(m + 1) * ROWS], 0.0), axis=0, keepdims=True)
        total += values_ref[m:m + 1] * part
    out_ref[...] = jnp.concatenate([total[:, i * 128:(i + 1) * 128] for i in range(SLOTS // 128)], axis=0)


def spread(count_ref, parts_ref, weight_ref, basis_ref, values_ref, index_ref, out_ref):
    sampled = jnp.sum(parts_ref[...], axis=0)
    sampled = jnp.concatenate([sampled[i:i + 1] for i in range(SLOTS // 128)], axis=1)
    usable = lax.broadcasted_iota(i32, (1, SLOTS), 1) < count_ref[0]
    weighted = jnp.where(usable, (weight_ref[...] * (SCALE * SCALE)) * sampled, 0.0)
    line, _ = cell_parts(index_ref)
    row = jnp.where(line >= ROWS, line - ROWS, line)
    mine = lax.broadcasted_iota(i32, (ROWS, SLOTS), 0) == row
    highs, lows = [], []
    for m in range(LOCAL_M):
        value = values_ref[m:m + 1] * weighted
        high = value.astype(bf16).astype(f32)
        highs.append(jnp.where(mine, high, 0.0).astype(bf16))
        lows.append(jnp.where(mine, value - high, 0.0).astype(bf16))
    empty = jnp.zeros((32, SLOTS), bf16)
    right = jnp.concatenate(highs + [empty] + lows + [empty], axis=0)
    nt = ((1,), (1,))
    both = dot(basis_ref[0], right, nt)
    result = both[:, :128] + both[:, 128:] + dot(basis_ref[1], right[:128], nt)
    wide = LOCAL_M * ROWS
    pieces = [result[k * N_SP:(k + 1) * N_SP, :wide] for k in range(LOCAL_KB)]
    out_ref[:, 0, :] = jnp.concatenate(pieces, axis=1)


def fold(x):
    x = jnp.sum(x, axis=0, keepdims=True)
    return x[:, :128] + x[:, 128:256] + x[:, 256:384] + x[:, 384:]


def from_rows(recv_ref, phase_ref, rows_ref, amp_ref, dir_ref, grad_ref, prod_ref, sums_ref):
    count = LOCAL_M * LOCAL_KB
    recv = recv_ref[:, 0, :]
    high, low = split(recv)
    left = []
    for i in range(count):
        at = slice(i * ROWS, (i + 1) * ROWS)
        left.append(jnp.concatenate([high[:, at], low[:, at], high[:, at]], axis=1))
    table_high, table_low = split(rows_ref[...])
    table = jnp.concatenate([table_high, table_high, table_low], axis=0)
    turned = dot(jnp.concatenate(left, axis=0), table, ((1,), (0,)))
    phase_c, phase_s = phase_ref[0], phase_ref[1]
    amp = amp_ref[...]
    totals = [jnp.zeros((1, 128), f32)] * 4
    for m in range(LOCAL_M):
        part_c, part_s = [], []
        for k in range(LOCAL_KB):
            i = k * LOCAL_M + m
            p, q = turned[i * N_SP:(i + 1) * N_SP, :KA], turned[i * N_SP:(i + 1) * N_SP, KA:]
            part_c.append(jnp.sum(p * phase_c - q * phase_s, axis=0, keepdims=True))
            part_s.append(jnp.sum(p * phase_s + q * phase_c, axis=0, keepdims=True))
        back_c = jnp.concatenate(part_c, axis=0)
        back_s = pltpu.roll(jnp.concatenate(part_s, axis=0), KA - 1, 1)
        d, g = dir_ref[m], grad_ref[m]
        product = d + amp * jnp.concatenate([back_c, back_s], axis=1)
        prod_ref[m] = product
        terms = (g * g, d * product, g * product, product * product)
        totals = [t + fold(x) for t, x in zip(totals, terms)]
    lane = lax.broadcasted_iota(i32, (1, 128), 1)
    line = jnp.zeros((1, 128), f32)
    for k, t in enumerate(totals):
        t = t + pltpu.roll(t, 64, 1)
        t = t + pltpu.roll(t, 32, 1)
        line = jnp.where((lane >> 5) == k, t, line)
    sums_ref[...] = line


def update(parts_ref, cont_ref, grad_ref, dir_ref, prod_ref, cont_out, grad_out, dir_out):
    line = jnp.sum(parts_ref[...], axis=0)
    group = lax.broadcasted_iota(i32, (1, 128), 1) >> 5
    grad_sq, curvature, cross, prod_sq = [
        jnp.sum(jnp.where(group == k, line, 0.0), axis=1, keepdims=True) for k in range(4)]
    step = grad_sq / curvature
    new_sq = grad_sq + step * (2.0 * cross + step * prod_sq)
    ratio = new_sq / grad_sq
    for m in range(LOCAL_M):
        d = dir_ref[m]
        fresh = grad_ref[m] + step * prod_ref[m]
        cont_out[m] = cont_ref[m] + step * d
        grad_out[m] = fresh
        dir_out[m] = ratio * d - fresh


def call(kernel, in_specs, outs, scratch=(), flops=0, moved=0, params=PARAMS):
    shapes = [jax.ShapeDtypeStruct(shape, dtype) for shape, dtype in outs]
    return pl.pallas_call(
        kernel,
        out_shape=shapes,
        in_specs=in_specs,
        out_specs=[VMEM] * len(shapes),
        scratch_shapes=list(scratch),
        compiler_params=params,
        cost_estimate=pl.CostEstimate(flops=flops, bytes_accessed=moved, transcendentals=0),
    )


def stage_to_rows(pencil, cutoff, direction):
    return call(
        to_rows, [SMEM, SMEM, HBM],
        [((N_SP, 1, CHUNK), f32), ((LOCAL_KB, 2 * KA), f32)],
        [pltpu.VMEM((8 * N_SP, 2 * KA), bf16), pltpu.VMEM((8 * N_SP, 2 * KA), bf16),
         pltpu.VMEM((LOCAL_M, LOCAL_KB, 2 * KA), f32), pltpu.SemaphoreType.DMA],
        flops=10 ** 8, moved=10 ** 6, params=WHOLE,
    )(pencil, cutoff, direction)


def stage_at_slots(index, perturb):
    return call(
        at_slots, [VMEM] * 2,
        [((2, 2 * KB, SLOTS), bf16), ((LOCAL_M, SLOTS), f32)],
        flops=2 * 10 ** 9, moved=4 * 10 ** 6,
    )(index, perturb)


def stage_sample(recv, basis, values, index):
    return call(
        sample, [VMEM] * 4, [((SLOTS // 128, 128), f32)], flops=3 * 10 ** 8, moved=2 * 10 ** 6,
    )(recv, basis, values, index)[0]


def stage_spread(count, parts, weight, basis, values, index):
    return call(
        spread, [SMEM] + [VMEM] * 5, [((N_SP, 1, CHUNK), f32)], flops=3 * 10 ** 8, moved=2 * 10 ** 6,
    )(count, parts, weight, basis, values, index)[0]


def stage_from_rows(recv, phase, rows, amp, direction, gradient):
    return call(
        from_rows, [VMEM] * 6,
        [((LOCAL_M, LOCAL_KB, 2 * KA), f32), ((1, 128), f32)],
        flops=10 ** 8, moved=10 ** 6,
    )(recv, phase, rows, amp, direction, gradient)


def stage_update(parts, control, gradient, direction, product):
    shape = (LOCAL_M, LOCAL_KB, 2 * KA)
    return call(
        update, [VMEM] * 5, [(shape, f32)] * 3, flops=10 ** 5, moved=10 ** 5,
    )(parts, control, gradient, direction, product)


NEAR = [[m * N_SP + s + y for m in range(SIDE) for y in range(2)] for s in range(0, N_SP, 2)]
FAR = [[m * N_SP + s + y for s in range(0, N_SP, 2)] for m in range(SIDE) for y in range(2)]


def swap(x):
    return lax.all_to_all(x, "sp", 0, 0, tiled=True)


def share(x, axis, count, groups=None):
    x = jnp.broadcast_to(x[None], (count,) + x.shape)
    return lax.all_to_all(x, axis, 0, 0, axis_index_groups=groups, tiled=True)


def shards(phase, rows, control, gradient, direction, perturb, obs_index, obs_count, obs_weight, cutoff):
    pencil = lax.axis_index("sp").astype(i32).reshape(1)
    send, amp = stage_to_rows(pencil, cutoff, direction)
    basis, values = stage_at_slots(obs_index, perturb.reshape(LOCAL_M * LEVELS * ROWS, NB))
    part = stage_sample(swap(send), basis, values, obs_index)
    send = stage_spread(obs_count, share(part, "mem", SIDE), obs_weight, basis, values, obs_index)
    product, sums = stage_from_rows(swap(send), phase, rows, amp, direction, gradient)
    sums = jnp.sum(share(sums, ("mem", "sp"), len(NEAR[0]), NEAR), axis=0)
    sums = share(sums, ("mem", "sp"), len(FAR[0]), FAR)
    return tuple(stage_update(sums, control, gradient, direction, product))


def solution(mesh):
    spectral = P("mem", "sp", None)
    placed = (spectral, spectral, spectral, P("mem", None, "sp", None), P("sp", None), P("sp"), P("sp", None), P())
    phase, rows = tables()
    return jax.shard_map(
        functools.partial(shards, phase, rows),
        mesh=mesh,
        in_specs=placed,
        out_specs=(spectral, spectral, spectral),
        check_vma=False,
    )
```

```python
import functools
import math

import jax
import jax.numpy as jnp
import numpy as np
from jax import lax
from jax.experimental import pallas as pl
from jax.experimental.pallas import tpu as pltpu
from jax.sharding import PartitionSpec as P

NA, NB, KA, KB = 3072, 1536, 256, 128
LEVELS, SLOTS, MEMBERS, ROWS, N_SP = 2, 2048, 16, 48, 64
LOCAL_M, LOCAL_KB = 2, 4
SIDE = 8
SCALE = 1.0 / math.sqrt(MEMBERS - 1)
CHUNK = LOCAL_KB * LOCAL_M * ROWS

f32, bf16, i32 = jnp.float32, jnp.bfloat16, jnp.int32
VMEM = pl.BlockSpec(memory_space=pltpu.VMEM)
HBM = pl.BlockSpec(memory_space=pltpu.HBM)
SMEM = pl.BlockSpec(memory_space=pltpu.SMEM)
PARAMS = pltpu.CompilerParams(vmem_limit_bytes=40 * 1024 * 1024)
WHOLE = pltpu.CompilerParams(vmem_limit_bytes=60 * 1024 * 1024)


def tables():
    w = np.arange(KA, dtype=np.int64)
    s = np.arange(N_SP, dtype=np.int64)[:, None]
    turn = 2.0 * np.pi * ((s * w) % N_SP) / N_SP
    r = np.arange(ROWS, dtype=np.int64)[:, None]
    ws = np.where(w == 0, KA, w)
    cos_rows = np.cos(2.0 * np.pi * ((r * w) % NA) / NA)
    sin_rows = np.sin(2.0 * np.pi * ((r * ws) % NA) / NA)
    rows = np.concatenate([cos_rows, sin_rows], axis=1).astype(np.float32)
    phase = np.stack([np.cos(turn), np.sin(turn)]).astype(np.float32)
    return phase, rows


def split(x):
    high = x.astype(bf16)
    return high, (x - high.astype(f32)).astype(bf16)


def dot(a, b, dims):
    return lax.dot_general(a, b, (dims, ((), ())), preferred_element_type=f32)


def wave(column, modes):
    return jnp.where(column < modes, column, column - modes + 1)


def shape_factor(radius, cutoff):
    retained = 4096 * radius <= cutoff * cutoff * (KA * KA)
    factor = 1.0 / (1.0 + (16.0 / (KA * KA)) * radius.astype(f32))
    return jnp.where(retained, factor, 0.0)


def to_rows(pen_ref, cut_ref, dir_in, out_ref, amp_ref, high_ref, low_ref, dir_ref, sem):
    dir_copy = pltpu.make_async_copy(dir_in, dir_ref, sem)
    dir_copy.start()
    w = lax.broadcasted_iota(i32, (1, 128), 1)
    s = lax.broadcasted_iota(i32, (N_SP, 1), 0)
    phase_c, phase_s = turns_to_cos_sin(((s * w) & (N_SP - 1)).astype(f32) * (1.0 / N_SP))
    phase_c = jnp.concatenate([phase_c, phase_c], axis=1)
    phase_s = jnp.concatenate([phase_s, phase_s], axis=1)
    r = lax.broadcasted_iota(i32, (ROWS, 1), 0)
    w = lax.broadcasted_iota(i32, (1, KA), 1)
    ws = jnp.where(w == 0, KA, w)
    cos_r, sin_r = turns_to_cos_sin(residue_turns(ws.astype(f32), r.astype(f32), NA))
    table_high, table_low = split(jnp.concatenate([jnp.where(w == 0, 1.0, cos_r), sin_r], axis=1))
    cutoff, pencil = cut_ref[0], pen_ref[0]
    wa = lax.broadcasted_iota(i32, (1, 384), 1)
    wb = lax.broadcasted_iota(i32, (136, 1), 0)
    count_a = jnp.where(wa > KA, 0.0, jnp.where((wa == 0) | (wa == KA), 1.0, 2.0))
    count_b = jnp.where(wb > KB, 0.0, jnp.where((wb == 0) | (wb == KB), 1.0, 2.0))
    factor = shape_factor(wa * wa + 4 * (wb * wb), cutoff)
    energy = jnp.sum(factor * factor * count_a * count_b, axis=0, keepdims=True)
    energy = jnp.sum(energy, axis=1, keepdims=True)
    gain = jnp.sqrt(2.0 / energy)
    wa = wave(lax.broadcasted_iota(i32, (1, 2 * KA), 1), KA)
    wb = wave(lax.broadcasted_iota(i32, (LOCAL_KB, 1), 0) + pencil * LOCAL_KB, KB)
    amp = shape_factor(wa * wa + 4 * (wb * wb), cutoff) * gain
    amp_ref[...] = amp

    dir_copy.wait()
    nt = ((1,), (1,))
    pieces = [None] * (LOCAL_M * LOCAL_KB)
    for m in range(LOCAL_M):
        spectral = amp * dir_ref[m]
        part_c = spectral[:, :KA]
        part_s = pltpu.roll(spectral[:, KA:], 1, 1)
        for k in range(LOCAL_KB):
            c, s = part_c[k:k + 1], part_s[k:k + 1]
            at = pl.ds((m * LOCAL_KB + k) * N_SP, N_SP)
            for half, value in ((0, c * phase_c + s * phase_s), (1, s * phase_c - c * phase_s)):
                high, low = split(value)
                high_ref[at, half * KA:(half + 1) * KA] = high
                low_ref[at, half * KA:(half + 1) * KA] = low
        of_m = pl.ds(m * LOCAL_KB * N_SP, LOCAL_KB * N_SP)
        result = (dot(high_ref[of_m], table_high, nt) + dot(high_ref[of_m], table_low, nt)
                  + dot(low_ref[of_m], table_high, nt))
        for k in range(LOCAL_KB):
            pieces[k * LOCAL_M + m] = result[k * N_SP:(k + 1) * N_SP]
    out_ref[:, 0, :] = jnp.concatenate(pieces, axis=1)


def cell_parts(index_ref):
    index = index_ref[...]
    line = jnp.floor((index.astype(f32) + 0.5) * (1.0 / NB)).astype(i32)
    column = index - line * NB
    return line, column


def turns_to_cos_sin(turns):
    quarter = jnp.floor(turns * 4.0 + 0.5)
    x = (turns - quarter * 0.25) * (2.0 * math.pi)
    x2 = x * x
    s = x * (1.0 + x2 * (-1.0 / 6 + x2 * (1.0 / 120 + x2 * (-1.0 / 5040 + x2 * (1.0 / 362880)))))
    c = 1.0 + x2 * (-0.5 + x2 * (1.0 / 24 + x2 * (-1.0 / 720 + x2 * (1.0 / 40320))))
    q = quarter.astype(i32) & 3
    odd = (q & 1) == 1
    cos = jnp.where(odd, s, c)
    sin = jnp.where(odd, c, s)
    return jnp.where((q == 1) | (q == 2), -cos, cos), jnp.where(q >= 2, -sin, sin)


def residue_turns(wavenum, place, length):
    product = wavenum * place
    return (product - jnp.floor(product * (1.0 / length)) * length) * (1.0 / length)


def at_slots(index_ref, pert_ref, basis_ref, values_ref):
    block = 256

    @pl.loop(0, SLOTS // block)
    def _(step):
        at = pl.ds(pl.multiple_of(step * block, block), block)
        index = index_ref[:, at]
        line = jnp.floor((index.astype(f32) + 0.5) * (1.0 / NB)).astype(i32)
        column = index - line * NB
        place = column.astype(f32)
        y = lax.broadcasted_iota(i32, (SIDE, 1), 0)
        cos_y, sin_y = turns_to_cos_sin(residue_turns((4 * y).astype(f32), place, NB))
        q = lax.broadcasted_iota(i32, (SIDE * LOCAL_KB, 1), 0)
        is_sin = (q & 7) >= SIDE // 2
        wq = (32 * (q & 3) + (q >> 3) + is_sin.astype(i32)).astype(f32)
        cos_q, sin_q = turns_to_cos_sin(residue_turns(wq, place, NB) - jnp.where(is_sin, 0.25, 0.0))
        for pair in range(SIDE * LOCAL_KB // 2):
            both = [cos_y * cos_q[g:g + 1] - sin_y * sin_q[g:g + 1] for g in (2 * pair, 2 * pair + 1)]
            high, low = split(jnp.concatenate(both, axis=0))
            basis_ref[0, pair * 16:(pair + 1) * 16, at] = high
            basis_ref[1, pair * 16:(pair + 1) * 16, at] = low
        lines = LEVELS * ROWS
        grid_column = lax.broadcasted_iota(i32, (NB, block), 0)
        chosen = jnp.where(grid_column == column, 1.0, 0.0).astype(bf16)
        found = dot(pert_ref[...], chosen, ((1,), (0,)))
        mine = lax.broadcasted_iota(i32, (lines, block), 0) == line
        for m in range(LOCAL_M):
            part = jnp.where(mine, found[m * lines:(m + 1) * lines], 0.0)
            values_ref[m:m + 1, at] = jnp.sum(part, axis=0, keepdims=True)


def sample(recv_ref, basis_ref, values_ref, index_ref, out_ref):
    wide = LOCAL_M * ROWS
    recv = recv_ref[:, 0, :]
    field = jnp.concatenate([recv[:, k * wide:(k + 1) * wide] for k in range(LOCAL_KB)], axis=0)
    high, low = split(field.T)
    nn = ((1,), (0,))
    both = dot(jnp.concatenate([high, low], axis=0), basis_ref[0], nn)
    rows = both[:wide] + both[wide:] + dot(high, basis_ref[1], nn)
    line, _ = cell_parts(index_ref)
    row = jnp.where(line >= ROWS, line - ROWS, line)
    mine = lax.broadcasted_iota(i32, (ROWS, SLOTS), 0) == row
    total = jnp.zeros((1, SLOTS), f32)
    for m in range(LOCAL_M):
        part = jnp.sum(jnp.where(mine, rows[m * ROWS:(m + 1) * ROWS], 0.0), axis=0, keepdims=True)
        total += values_ref[m:m + 1] * part
    out_ref[...] = jnp.concatenate([total[:, i * 128:(i + 1) * 128] for i in range(SLOTS // 128)], axis=0)


def spread(count_ref, parts_ref, weight_ref, basis_ref, values_ref, index_ref, out_ref):
    sampled = jnp.sum(parts_ref[...], axis=0)
    sampled = jnp.concatenate([sampled[i:i + 1] for i in range(SLOTS // 128)], axis=1)
    usable = lax.broadcasted_iota(i32, (1, SLOTS), 1) < count_ref[0]
    weighted = jnp.where(usable, (weight_ref[...] * (SCALE * SCALE)) * sampled, 0.0)
    line, _ = cell_parts(index_ref)
    row = jnp.where(line >= ROWS, line - ROWS, line)
    mine = lax.broadcasted_iota(i32, (ROWS, SLOTS), 0) == row
    highs, lows = [], []
    for m in range(LOCAL_M):
        value = values_ref[m:m + 1] * weighted
        high = value.astype(bf16).astype(f32)
        highs.append(jnp.where(mine, high, 0.0).astype(bf16))
        lows.append(jnp.where(mine, value - high, 0.0).astype(bf16))
    empty = jnp.zeros((32, SLOTS), bf16)
    right = jnp.concatenate(highs + [empty] + lows + [empty], axis=0)
    nt = ((1,), (1,))
    both = dot(basis_ref[0], right, nt)
    result = both[:, :128] + both[:, 128:] + dot(basis_ref[1], right[:128], nt)
    wide = LOCAL_M * ROWS
    pieces = [result[k * N_SP:(k + 1) * N_SP, :wide] for k in range(LOCAL_KB)]
    out_ref[:, 0, :] = jnp.concatenate(pieces, axis=1)


def fold(x):
    x = jnp.sum(x, axis=0, keepdims=True)
    return x[:, :128] + x[:, 128:256] + x[:, 256:384] + x[:, 384:]


def from_rows(recv_ref, phase_ref, rows_ref, amp_ref, dir_ref, grad_ref, prod_ref, sums_ref):
    count = LOCAL_M * LOCAL_KB
    recv = recv_ref[:, 0, :]
    high, low = split(recv)
    left = []
    for i in range(count):
        at = slice(i * ROWS, (i + 1) * ROWS)
        left.append(jnp.concatenate([high[:, at], low[:, at], high[:, at]], axis=1))
    table_high, table_low = split(rows_ref[...])
    table = jnp.concatenate([table_high, table_high, table_low], axis=0)
    turned = dot(jnp.concatenate(left, axis=0), table, ((1,), (0,)))
    phase_c, phase_s = phase_ref[0], phase_ref[1]
    amp = amp_ref[...]
    totals = [jnp.zeros((1, 128), f32)] * 4
    for m in range(LOCAL_M):
        part_c, part_s = [], []
        for k in range(LOCAL_KB):
            i = k * LOCAL_M + m
            p, q = turned[i * N_SP:(i + 1) * N_SP, :KA], turned[i * N_SP:(i + 1) * N_SP, KA:]
            part_c.append(jnp.sum(p * phase_c - q * phase_s, axis=0, keepdims=True))
            part_s.append(jnp.sum(p * phase_s + q * phase_c, axis=0, keepdims=True))
        back_c = jnp.concatenate(part_c, axis=0)
        back_s = pltpu.roll(jnp.concatenate(part_s, axis=0), KA - 1, 1)
        d, g = dir_ref[m], grad_ref[m]
        product = d + amp * jnp.concatenate([back_c, back_s], axis=1)
        prod_ref[m] = product
        terms = (g * g, d * product, g * product, product * product)
        totals = [t + fold(x) for t, x in zip(totals, terms)]
    lane = lax.broadcasted_iota(i32, (1, 128), 1)
    line = jnp.zeros((1, 128), f32)
    for k, t in enumerate(totals):
        t = t + pltpu.roll(t, 64, 1)
        t = t + pltpu.roll(t, 32, 1)
        line = jnp.where((lane >> 5) == k, t, line)
    sums_ref[...] = line


def update(parts_ref, cont_ref, grad_ref, dir_ref, prod_ref, cont_out, grad_out, dir_out):
    line = jnp.sum(parts_ref[...], axis=0)
    group = lax.broadcasted_iota(i32, (1, 128), 1) >> 5
    grad_sq, curvature, cross, prod_sq = [
        jnp.sum(jnp.where(group == k, line, 0.0), axis=1, keepdims=True) for k in range(4)]
    step = grad_sq / curvature
    new_sq = grad_sq + step * (2.0 * cross + step * prod_sq)
    ratio = new_sq / grad_sq
    for m in range(LOCAL_M):
        d = dir_ref[m]
        fresh = grad_ref[m] + step * prod_ref[m]
        cont_out[m] = cont_ref[m] + step * d
        grad_out[m] = fresh
        dir_out[m] = ratio * d - fresh


def call(kernel, in_specs, outs, scratch=(), flops=0, moved=0, params=PARAMS):
    shapes = [jax.ShapeDtypeStruct(shape, dtype) for shape, dtype in outs]
    return pl.pallas_call(
        kernel,
        out_shape=shapes,
        in_specs=in_specs,
        out_specs=[VMEM] * len(shapes),
        scratch_shapes=list(scratch),
        compiler_params=params,
        cost_estimate=pl.CostEstimate(flops=flops, bytes_accessed=moved, transcendentals=0),
    )


def stage_to_rows(pencil, cutoff, direction):
    return call(
        to_rows, [SMEM, SMEM, HBM],
        [((N_SP, 1, CHUNK), f32), ((LOCAL_KB, 2 * KA), f32)],
        [pltpu.VMEM((8 * N_SP, 2 * KA), bf16), pltpu.VMEM((8 * N_SP, 2 * KA), bf16),
         pltpu.VMEM((LOCAL_M, LOCAL_KB, 2 * KA), f32), pltpu.SemaphoreType.DMA],
        flops=10 ** 8, moved=10 ** 6, params=WHOLE,
    )(pencil, cutoff, direction)


def stage_at_slots(index, perturb):
    return call(
        at_slots, [VMEM] * 2,
        [((2, 2 * KB, SLOTS), bf16), ((LOCAL_M, SLOTS), f32)],
        flops=2 * 10 ** 9, moved=4 * 10 ** 6,
    )(index, perturb)


def stage_sample(recv, basis, values, index):
    return call(
        sample, [VMEM] * 4, [((SLOTS // 128, 128), f32)], flops=3 * 10 ** 8, moved=2 * 10 ** 6,
    )(recv, basis, values, index)[0]


def stage_spread(count, parts, weight, basis, values, index):
    return call(
        spread, [SMEM] + [VMEM] * 5, [((N_SP, 1, CHUNK), f32)], flops=3 * 10 ** 8, moved=2 * 10 ** 6,
    )(count, parts, weight, basis, values, index)[0]


def stage_from_rows(recv, phase, rows, amp, direction, gradient):
    return call(
        from_rows, [VMEM] * 6,
        [((LOCAL_M, LOCAL_KB, 2 * KA), f32), ((1, 128), f32)],
        flops=10 ** 8, moved=10 ** 6,
    )(recv, phase, rows, amp, direction, gradient)


def stage_update(parts, control, gradient, direction, product):
    shape = (LOCAL_M, LOCAL_KB, 2 * KA)
    return call(
        update, [VMEM] * 5, [(shape, f32)] * 3, flops=10 ** 5, moved=10 ** 5,
    )(parts, control, gradient, direction, product)


def swap(x):
    return lax.all_to_all(x, "sp", 0, 0, tiled=True)


def share(x, axis, count):
    x = jnp.broadcast_to(x[None], (count,) + x.shape)
    return lax.all_to_all(x, axis, 0, 0, tiled=True)


def shards(phase, rows, control, gradient, direction, perturb, obs_index, obs_count, obs_weight, cutoff):
    pencil = lax.axis_index("sp").astype(i32).reshape(1)
    send, amp = stage_to_rows(pencil, cutoff, direction)
    basis, values = stage_at_slots(obs_index, perturb.reshape(LOCAL_M * LEVELS * ROWS, NB))
    part = stage_sample(swap(send), basis, values, obs_index)
    send = stage_spread(obs_count, share(part, "mem", SIDE), obs_weight, basis, values, obs_index)
    product, sums = stage_from_rows(swap(send), phase, rows, amp, direction, gradient)
    sums = jnp.sum(share(sums, "mem", SIDE), axis=0)
    sums = share(sums, "sp", N_SP)
    return tuple(stage_update(sums, control, gradient, direction, product))


def solution(mesh):
    spectral = P("mem", "sp", None)
    placed = (spectral, spectral, spectral, P("mem", None, "sp", None), P("sp", None), P("sp"), P("sp", None), P())
    phase, rows = tables()
    return jax.shard_map(
        functools.partial(shards, phase, rows),
        mesh=mesh,
        in_specs=placed,
        out_specs=(spectral, spectral, spectral),
        check_vma=False,
    )
```

```python
import functools
import math

import jax
import jax.numpy as jnp
import numpy as np
from jax import lax
from jax.experimental import pallas as pl
from jax.experimental.pallas import tpu as pltpu
from jax.sharding import PartitionSpec as P

NA, NB, KA, KB = 3072, 1536, 256, 128
LEVELS, SLOTS, MEMBERS, ROWS, N_SP = 2, 2048, 16, 48, 64
LOCAL_M, LOCAL_KB = 2, 4
SIDE = 8
SCALE = 1.0 / math.sqrt(MEMBERS - 1)
CHUNK = LOCAL_KB * LOCAL_M * ROWS

f32, bf16, i32 = jnp.float32, jnp.bfloat16, jnp.int32
VMEM = pl.BlockSpec(memory_space=pltpu.VMEM)
HBM = pl.BlockSpec(memory_space=pltpu.HBM)
SMEM = pl.BlockSpec(memory_space=pltpu.SMEM)
PARAMS = pltpu.CompilerParams(vmem_limit_bytes=40 * 1024 * 1024)
WHOLE = pltpu.CompilerParams(vmem_limit_bytes=60 * 1024 * 1024)


def tables():
    w = np.arange(KA, dtype=np.int64)
    s = np.arange(N_SP, dtype=np.int64)[:, None]
    turn = 2.0 * np.pi * ((s * w) % N_SP) / N_SP
    r = np.arange(ROWS, dtype=np.int64)[:, None]
    ws = np.where(w == 0, KA, w)
    cos_rows = np.cos(2.0 * np.pi * ((r * w) % NA) / NA)
    sin_rows = np.sin(2.0 * np.pi * ((r * ws) % NA) / NA)
    rows = np.concatenate([cos_rows, sin_rows], axis=1).astype(np.float32)
    phase = np.stack([np.cos(turn), np.sin(turn)]).astype(np.float32)
    return phase, rows


def split(x):
    high = x.astype(bf16)
    return high, (x - high.astype(f32)).astype(bf16)


def dot(a, b, dims):
    return lax.dot_general(a, b, (dims, ((), ())), preferred_element_type=f32)


def wave(column, modes):
    return jnp.where(column < modes, column, column - modes + 1)


def shape_factor(radius, cutoff):
    retained = 4096 * radius <= cutoff * cutoff * (KA * KA)
    factor = 1.0 / (1.0 + (16.0 / (KA * KA)) * radius.astype(f32))
    return jnp.where(retained, factor, 0.0)


def to_rows(pen_ref, cut_ref, dir_in, out_ref, amp_ref, high_ref, low_ref, dir_ref, sem):
    dir_copy = pltpu.make_async_copy(dir_in, dir_ref, sem)
    dir_copy.start()
    w = lax.broadcasted_iota(i32, (1, 128), 1)
    s = lax.broadcasted_iota(i32, (N_SP, 1), 0)
    phase_c, phase_s = turns_to_cos_sin(((s * w) & (N_SP - 1)).astype(f32) * (1.0 / N_SP))
    phase_c = jnp.concatenate([phase_c, phase_c], axis=1)
    phase_s = jnp.concatenate([phase_s, phase_s], axis=1)
    r = lax.broadcasted_iota(i32, (ROWS, 1), 0)
    w = lax.broadcasted_iota(i32, (1, KA), 1)
    ws = jnp.where(w == 0, KA, w)
    cos_r, sin_r = turns_to_cos_sin(residue_turns(ws.astype(f32), r.astype(f32), NA))
    table_high, table_low = split(jnp.concatenate([jnp.where(w == 0, 1.0, cos_r), sin_r], axis=1))
    empty = jnp.zeros((128 - ROWS, 2 * KA), bf16)
    table_both = jnp.concatenate([table_high, empty, table_low, empty], axis=0)
    cutoff, pencil = cut_ref[0], pen_ref[0]
    wa = lax.broadcasted_iota(i32, (1, 384), 1)
    wb = lax.broadcasted_iota(i32, (136, 1), 0)
    count_a = jnp.where(wa > KA, 0.0, jnp.where((wa == 0) | (wa == KA), 1.0, 2.0))
    count_b = jnp.where(wb > KB, 0.0, jnp.where((wb == 0) | (wb == KB), 1.0, 2.0))
    factor = shape_factor(wa * wa + 4 * (wb * wb), cutoff)
    energy = jnp.sum(factor * factor * count_a * count_b, axis=0, keepdims=True)
    energy = jnp.sum(energy, axis=1, keepdims=True)
    gain = jnp.sqrt(2.0 / energy)
    wa = wave(lax.broadcasted_iota(i32, (1, 2 * KA), 1), KA)
    wb = wave(lax.broadcasted_iota(i32, (LOCAL_KB, 1), 0) + pencil * LOCAL_KB, KB)
    amp = shape_factor(wa * wa + 4 * (wb * wb), cutoff) * gain
    amp_ref[...] = amp

    dir_copy.wait()
    nt = ((1,), (1,))
    pieces = [None] * (LOCAL_M * LOCAL_KB)
    for m in range(LOCAL_M):
        spectral = amp * dir_ref[m]
        part_c = spectral[:, :KA]
        part_s = pltpu.roll(spectral[:, KA:], 1, 1)
        for k in range(LOCAL_KB):
            c, s = part_c[k:k + 1], part_s[k:k + 1]
            at = pl.ds((m * LOCAL_KB + k) * N_SP, N_SP)
            for half, value in ((0, c * phase_c + s * phase_s), (1, s * phase_c - c * phase_s)):
                high, low = split(value)
                high_ref[at, half * KA:(half + 1) * KA] = high
                low_ref[at, half * KA:(half + 1) * KA] = low
        of_m = pl.ds(m * LOCAL_KB * N_SP, LOCAL_KB * N_SP)
        both = dot(high_ref[of_m], table_both, nt)
        result = both[:, :ROWS] + both[:, 128:128 + ROWS] + dot(low_ref[of_m], table_high, nt)
        for k in range(LOCAL_KB):
            pieces[k * LOCAL_M + m] = result[k * N_SP:(k + 1) * N_SP]
    out_ref[:, 0, :] = jnp.concatenate(pieces, axis=1)


def cell_parts(index_ref):
    index = index_ref[...]
    line = jnp.floor((index.astype(f32) + 0.5) * (1.0 / NB)).astype(i32)
    column = index - line * NB
    return line, column


def turns_to_cos_sin(turns):
    quarter = jnp.floor(turns * 4.0 + 0.5)
    x = (turns - quarter * 0.25) * (2.0 * math.pi)
    x2 = x * x
    s = x * (1.0 + x2 * (-1.0 / 6 + x2 * (1.0 / 120 + x2 * (-1.0 / 5040 + x2 * (1.0 / 362880)))))
    c = 1.0 + x2 * (-0.5 + x2 * (1.0 / 24 + x2 * (-1.0 / 720 + x2 * (1.0 / 40320))))
    q = quarter.astype(i32) & 3
    odd = (q & 1) == 1
    cos = jnp.where(odd, s, c)
    sin = jnp.where(odd, c, s)
    return jnp.where((q == 1) | (q == 2), -cos, cos), jnp.where(q >= 2, -sin, sin)


def residue_turns(wavenum, place, length):
    product = wavenum * place
    return (product - jnp.floor(product * (1.0 / length)) * length) * (1.0 / length)


def at_slots(index_ref, pert_ref, basis_ref, values_ref):
    block = 256

    @pl.loop(0, SLOTS // block)
    def _(step):
        at = pl.ds(pl.multiple_of(step * block, block), block)
        index = index_ref[:, at]
        line = jnp.floor((index.astype(f32) + 0.5) * (1.0 / NB)).astype(i32)
        column = index - line * NB
        place = column.astype(f32)
        y = lax.broadcasted_iota(i32, (SIDE, 1), 0)
        cos_y, sin_y = turns_to_cos_sin(residue_turns((4 * y).astype(f32), place, NB))
        q = lax.broadcasted_iota(i32, (SIDE * LOCAL_KB, 1), 0)
        is_sin = (q & 7) >= SIDE // 2
        wq = (32 * (q & 3) + (q >> 3) + is_sin.astype(i32)).astype(f32)
        cos_q, sin_q = turns_to_cos_sin(residue_turns(wq, place, NB) - jnp.where(is_sin, 0.25, 0.0))
        for pair in range(SIDE * LOCAL_KB // 2):
            both = [cos_y * cos_q[g:g + 1] - sin_y * sin_q[g:g + 1] for g in (2 * pair, 2 * pair + 1)]
            high, low = split(jnp.concatenate(both, axis=0))
            basis_ref[0, pair * 16:(pair + 1) * 16, at] = high
            basis_ref[1, pair * 16:(pair + 1) * 16, at] = low
        lines = LEVELS * ROWS
        grid_column = lax.broadcasted_iota(i32, (NB, block), 0)
        chosen = jnp.where(grid_column == column, 1.0, 0.0).astype(bf16)
        found = dot(pert_ref[...], chosen, ((1,), (0,)))
        mine = lax.broadcasted_iota(i32, (lines, block), 0) == line
        for m in range(LOCAL_M):
            part = jnp.where(mine, found[m * lines:(m + 1) * lines], 0.0)
            values_ref[m:m + 1, at] = jnp.sum(part, axis=0, keepdims=True)


def sample(recv_ref, basis_ref, values_ref, index_ref, out_ref):
    wide = LOCAL_M * ROWS
    recv = recv_ref[:, 0, :]
    field = jnp.concatenate([recv[:, k * wide:(k + 1) * wide] for k in range(LOCAL_KB)], axis=0)
    high, low = split(field.T)
    nn = ((1,), (0,))
    both = dot(jnp.concatenate([high, low], axis=0), basis_ref[0], nn)
    rows = both[:wide] + both[wide:] + dot(high, basis_ref[1], nn)
    line, _ = cell_parts(index_ref)
    row = jnp.where(line >= ROWS, line - ROWS, line)
    mine = lax.broadcasted_iota(i32, (ROWS, SLOTS), 0) == row
    total = jnp.zeros((1, SLOTS), f32)
    for m in range(LOCAL_M):
        part = jnp.sum(jnp.where(mine, rows[m * ROWS:(m + 1) * ROWS], 0.0), axis=0, keepdims=True)
        total += values_ref[m:m + 1] * part
    out_ref[...] = jnp.concatenate([total[:, i * 128:(i + 1) * 128] for i in range(SLOTS // 128)], axis=0)


def spread(count_ref, parts_ref, weight_ref, basis_ref, values_ref, index_ref, out_ref):
    sampled = jnp.sum(parts_ref[...], axis=0)
    sampled = jnp.concatenate([sampled[i:i + 1] for i in range(SLOTS // 128)], axis=1)
    usable = lax.broadcasted_iota(i32, (1, SLOTS), 1) < count_ref[0]
    weighted = jnp.where(usable, (weight_ref[...] * (SCALE * SCALE)) * sampled, 0.0)
    line, _ = cell_parts(index_ref)
    row = jnp.where(line >= ROWS, line - ROWS, line)
    mine = lax.broadcasted_iota(i32, (ROWS, SLOTS), 0) == row
    highs, lows = [], []
    for m in range(LOCAL_M):
        value = values_ref[m:m + 1] * weighted
        high = value.astype(bf16).astype(f32)
        highs.append(jnp.where(mine, high, 0.0).astype(bf16))
        lows.append(jnp.where(mine, value - high, 0.0).astype(bf16))
    empty = jnp.zeros((32, SLOTS), bf16)
    right = jnp.concatenate(highs + [empty] + lows + [empty], axis=0)
    nt = ((1,), (1,))
    both = dot(basis_ref[0], right, nt)
    result = both[:, :128] + both[:, 128:] + dot(basis_ref[1], right[:128], nt)
    wide = LOCAL_M * ROWS
    pieces = [result[k * N_SP:(k + 1) * N_SP, :wide] for k in range(LOCAL_KB)]
    out_ref[:, 0, :] = jnp.concatenate(pieces, axis=1)


def fold(x):
    x = jnp.sum(x, axis=0, keepdims=True)
    return x[:, :128] + x[:, 128:256] + x[:, 256:384] + x[:, 384:]


def from_rows(recv_ref, phase_ref, rows_ref, amp_ref, dir_ref, grad_ref, prod_ref, sums_ref):
    count = LOCAL_M * LOCAL_KB
    recv = recv_ref[:, 0, :]
    high, low = split(recv)
    left = []
    for i in range(count):
        at = slice(i * ROWS, (i + 1) * ROWS)
        left.append(jnp.concatenate([high[:, at], low[:, at], high[:, at]], axis=1))
    table_high, table_low = split(rows_ref[...])
    table = jnp.concatenate([table_high, table_high, table_low], axis=0)
    turned = dot(jnp.concatenate(left, axis=0), table, ((1,), (0,)))
    phase_c, phase_s = phase_ref[0], phase_ref[1]
    amp = amp_ref[...]
    totals = [jnp.zeros((1, 128), f32)] * 4
    for m in range(LOCAL_M):
        part_c, part_s = [], []
        for k in range(LOCAL_KB):
            i = k * LOCAL_M + m
            p, q = turned[i * N_SP:(i + 1) * N_SP, :KA], turned[i * N_SP:(i + 1) * N_SP, KA:]
            part_c.append(jnp.sum(p * phase_c - q * phase_s, axis=0, keepdims=True))
            part_s.append(jnp.sum(p * phase_s + q * phase_c, axis=0, keepdims=True))
        back_c = jnp.concatenate(part_c, axis=0)
        back_s = pltpu.roll(jnp.concatenate(part_s, axis=0), KA - 1, 1)
        d, g = dir_ref[m], grad_ref[m]
        product = d + amp * jnp.concatenate([back_c, back_s], axis=1)
        prod_ref[m] = product
        terms = (g * g, d * product, g * product, product * product)
        totals = [t + fold(x) for t, x in zip(totals, terms)]
    lane = lax.broadcasted_iota(i32, (1, 128), 1)
    line = jnp.zeros((1, 128), f32)
    for k, t in enumerate(totals):
        t = t + pltpu.roll(t, 64, 1)
        t = t + pltpu.roll(t, 32, 1)
        line = jnp.where((lane >> 5) == k, t, line)
    sums_ref[...] = line


def update(parts_ref, cont_ref, grad_ref, dir_ref, prod_ref, cont_out, grad_out, dir_out):
    line = jnp.sum(parts_ref[...], axis=0)
    group = lax.broadcasted_iota(i32, (1, 128), 1) >> 5
    grad_sq, curvature, cross, prod_sq = [
        jnp.sum(jnp.where(group == k, line, 0.0), axis=1, keepdims=True) for k in range(4)]
    step = grad_sq / curvature
    new_sq = grad_sq + step * (2.0 * cross + step * prod_sq)
    ratio = new_sq / grad_sq
    for m in range(LOCAL_M):
        d = dir_ref[m]
        fresh = grad_ref[m] + step * prod_ref[m]
        cont_out[m] = cont_ref[m] + step * d
        grad_out[m] = fresh
        dir_out[m] = ratio * d - fresh


def call(kernel, in_specs, outs, scratch=(), flops=0, moved=0, params=PARAMS):
    shapes = [jax.ShapeDtypeStruct(shape, dtype) for shape, dtype in outs]
    return pl.pallas_call(
        kernel,
        out_shape=shapes,
        in_specs=in_specs,
        out_specs=[VMEM] * len(shapes),
        scratch_shapes=list(scratch),
        compiler_params=params,
        cost_estimate=pl.CostEstimate(flops=flops, bytes_accessed=moved, transcendentals=0),
    )


def stage_to_rows(pencil, cutoff, direction):
    return call(
        to_rows, [SMEM, SMEM, HBM],
        [((N_SP, 1, CHUNK), f32), ((LOCAL_KB, 2 * KA), f32)],
        [pltpu.VMEM((8 * N_SP, 2 * KA), bf16), pltpu.VMEM((8 * N_SP, 2 * KA), bf16),
         pltpu.VMEM((LOCAL_M, LOCAL_KB, 2 * KA), f32), pltpu.SemaphoreType.DMA],
        flops=10 ** 8, moved=10 ** 6, params=WHOLE,
    )(pencil, cutoff, direction)


def stage_at_slots(index, perturb):
    return call(
        at_slots, [VMEM] * 2,
        [((2, 2 * KB, SLOTS), bf16), ((LOCAL_M, SLOTS), f32)],
        flops=2 * 10 ** 9, moved=4 * 10 ** 6,
    )(index, perturb)


def stage_sample(recv, basis, values, index):
    return call(
        sample, [VMEM] * 4, [((SLOTS // 128, 128), f32)], flops=3 * 10 ** 8, moved=2 * 10 ** 6,
    )(recv, basis, values, index)[0]


def stage_spread(count, parts, weight, basis, values, index):
    return call(
        spread, [SMEM] + [VMEM] * 5, [((N_SP, 1, CHUNK), f32)], flops=3 * 10 ** 8, moved=2 * 10 ** 6,
    )(count, parts, weight, basis, values, index)[0]


def stage_from_rows(recv, phase, rows, amp, direction, gradient):
    return call(
        from_rows, [VMEM] * 6,
        [((LOCAL_M, LOCAL_KB, 2 * KA), f32), ((1, 128), f32)],
        flops=10 ** 8, moved=10 ** 6,
    )(recv, phase, rows, amp, direction, gradient)


def stage_update(parts, control, gradient, direction, product):
    shape = (LOCAL_M, LOCAL_KB, 2 * KA)
    return call(
        update, [VMEM] * 5, [(shape, f32)] * 3, flops=10 ** 5, moved=10 ** 5,
    )(parts, control, gradient, direction, product)


def swap(x):
    return lax.all_to_all(x, "sp", 0, 0, tiled=True)


def share(x, axis, count):
    x = jnp.broadcast_to(x[None], (count,) + x.shape)
    return lax.all_to_all(x, axis, 0, 0, tiled=True)


def shards(phase, rows, control, gradient, direction, perturb, obs_index, obs_count, obs_weight, cutoff):
    pencil = lax.axis_index("sp").astype(i32).reshape(1)
    send, amp = stage_to_rows(pencil, cutoff, direction)
    basis, values = stage_at_slots(obs_index, perturb.reshape(LOCAL_M * LEVELS * ROWS, NB))
    part = stage_sample(swap(send), basis, values, obs_index)
    send = stage_spread(obs_count, share(part, "mem", SIDE), obs_weight, basis, values, obs_index)
    product, sums = stage_from_rows(swap(send), phase, rows, amp, direction, gradient)
    sums = jnp.sum(share(sums, "mem", SIDE), axis=0)
    sums = share(sums, "sp", N_SP)
    return tuple(stage_update(sums, control, gradient, direction, product))


def solution(mesh):
    spectral = P("mem", "sp", None)
    placed = (spectral, spectral, spectral, P("mem", None, "sp", None), P("sp", None), P("sp"), P("sp", None), P())
    phase, rows = tables()
    return jax.shard_map(
        functools.partial(shards, phase, rows),
        mesh=mesh,
        in_specs=placed,
        out_specs=(spectral, spectral, spectral),
        check_vma=False,
    )
```
